128 devices in a mesh: ctx: 16 (over x, z_lo, core), head: 8 (over y, z_hi).
Axes of the slice: x: 4, y: 4, z: 4 (z_hi: 2, z_lo: 2; z = z_hi * 2 + z_lo), core: 2. Of those that a mesh axis runs over, the one named last changes fastest.
Arguments:
- queries: bfloat16 [4096, 32, 256], P('ctx', 'head'), may hold values from -5 to 5
- cache_keys: bfloat16 [8192, 32, 256], P('ctx', 'head'), may hold values from -5 to 5
- cache_values: bfloat16 [8192, 32, 256], P('ctx', 'head'), may hold values from -6 to 6
- positions: int32 [4096], replicated, may hold values from 0 to 8191, as said below
- doc_spans: int32 [4096, 2], replicated, may hold values from 0 to 64, as said below
- lambdas: float32 [32], P('head'), may hold values from 0.2 to 0.8
- norm_gain: float32 [32, 256], P('head'), may hold values from 0.5 to 1.5
- out_weight: bfloat16 [8192, 8192], P('head'), may hold values from -0.0625 to 0.0625
Outputs:
- mixed: bfloat16 [4096, 8192], P(('ctx', 'head'))
The draws below stay inside these ranges and needn't reach their ends.
Inputs may be any that keep to these rules, and one draw needn't show every extreme that they name: positions[q] >= 128 * doc_spans[q, 0], so every question sees at least one token. doc_spans[q, 0] < doc_spans[q, 1].
All inputs are finite; a program needn't handle non-finite values.
Results may differ from the reference program's by a relative error of at most 0.024.
Values may be sent and summed in bfloat16 or wider, within the bound.
A program may use at most 256 MiB of HBM per device.

```python
import math
import jax
import jax.numpy as jnp
from jax import lax

D = 8192
HEADS = 32
QK = 128
VW = 256
BLK = 128
TOKENS = 8192
NQ = 4096
NB = 64


def layout(key):
    key = jax.random.fold_in(key, 101)
    low_key, high_key, pos_key, pick_key = jax.random.split(key, 4)
    rows_at = jnp.arange(NQ, dtype=jnp.int32)
    first_pick = jax.random.randint(pick_key, (), 8, NQ, dtype=jnp.int32)
    second_pick = 8 + (first_pick - 8 + 1) % (NQ - 8)
    span_low = jax.random.randint(low_key, (NQ,), 0, NB // 4, dtype=jnp.int32)
    span_high = jax.random.randint(high_key, (NQ,), NB // 2 + 1, NB + 1, dtype=jnp.int32)
    span_low = jnp.where(rows_at == first_pick, 0, span_low)
    span_high = jnp.where(rows_at == first_pick, NB, span_high)
    lowest = span_low * BLK
    lowest = jnp.where(rows_at < 8, jnp.maximum(lowest, TOKENS // 2), lowest)
    picked = jax.random.randint(pos_key, (NQ,), lowest, TOKENS, dtype=jnp.int32)
    picked = jnp.where(rows_at == first_pick, 0, picked)
    picked = jnp.where(rows_at == second_pick, TOKENS - 1, picked)
    return (picked, jnp.stack([span_low, span_high], axis=1))


def draw_positions(key, part):
    picked, spans_drawn = layout(key)
    return picked


def draw_doc_spans(key, part):
    picked, spans_drawn = layout(key)
    return spans_drawn


def draw_queries(key, part):
    key = jax.random.fold_in(key, 11)
    drawn = jnp.clip(jax.random.normal(key, (NQ, HEADS, 2 * QK), jnp.float32), -5.0, 5.0)
    return drawn.astype(jnp.bfloat16)


def draw_cache_keys(key, part):
    key = jax.random.fold_in(key, 13)
    drawn = jnp.clip(jax.random.normal(key, (TOKENS, HEADS, 2 * QK), jnp.float32), -5.0, 5.0)
    return drawn.astype(jnp.bfloat16)


def block_scale(own_key, extent, cuts, low, largest):
    loudness = 1.0
    for position, shards_of in cuts:
        draws = jax.random.uniform(jax.random.fold_in(jax.random.fold_in(own_key, 6), position), (shards_of,), jnp.float32, low / len(cuts), largest / len(cuts))
        loudness = loudness * jnp.repeat(jnp.exp(draws), extent[position] // shards_of).reshape((-1,) + (1,) * (len(extent) - 1 - position))
    return loudness


def noise(stream_key, extent, spread, limit, pieces=(), kind=jnp.bfloat16):
    entries = spread * jax.random.normal(stream_key, extent, jnp.float32)
    if pieces:
        entries = entries * block_scale(stream_key, extent, pieces, -0.22, 0.18)
    return jnp.clip(entries, -limit, limit).astype(kind)


def setup_inputs(seed: int = 0) -> dict:
    key_list = jax.random.split(jax.random.key(seed), 9)
    queries = draw_queries(jax.random.fold_in(key_list[8], 71), 0)
    cache_keys = draw_cache_keys(jax.random.fold_in(key_list[8], 71), 0)
    cache_values = noise(key_list[2], (TOKENS, HEADS, VW), 1.0, 6.0, ((0, 16), (1, 8)))
    positions = draw_positions(jax.random.fold_in(key_list[8], 71), 0)
    doc_spans = draw_doc_spans(jax.random.fold_in(key_list[8], 71), 0)
    lambdas = jnp.clip(jnp.exp(math.log(0.8) - 1.3862944 * jax.random.uniform(key_list[5], (HEADS,), jnp.float32) ** block_scale(key_list[5], (HEADS,), ((0, 8),), -0.2, 0.2)), 0.2, 0.8)
    norm_gain = jnp.clip(1.0 + 0.1 * jax.random.normal(key_list[6], (HEADS, VW), jnp.float32), 0.5, 1.5)
    out_weight = noise(key_list[7], (HEADS * VW, D), (HEADS * VW) ** -0.5, 0.0625, ((0, 8),))
    return {"queries": queries, "cache_keys": cache_keys, "cache_values": cache_values, "positions": positions, "doc_spans": doc_spans, "lambdas": lambdas, "norm_gain": norm_gain, "out_weight": out_weight}


NEG_BIG = -1e+30
LAMBDA_INIT = 0.8
EPSILON = 1e-05

def allowed_mask(positions, doc_spans, offset, amount):
    tokens_at = offset + jnp.arange(amount, dtype=jnp.int32)
    return (tokens_at[None, :] <= positions[:, None]) & (tokens_at[None, :] >= doc_spans[:, 0:1] * BLK) & (tokens_at[None, :] < doc_spans[:, 1:2] * BLK)

def reference(queries, cache_keys, cache_values, positions, doc_spans, lambdas, norm_gain, out_weight):
    allowed = allowed_mask(positions, doc_spans, 0, TOKENS)
    factor = QK ** (-0.5)

    def one_head(head_idx):
        query_rows = queries[:, head_idx]
        key_rows = cache_keys[:, head_idx]
        value_rows = cache_values[:, head_idx]
        results = []
        for half_idx in range(2):
            query_half = query_rows[:, half_idx * QK:(half_idx + 1) * QK]
            key_half = key_rows[:, half_idx * QK:(half_idx + 1) * QK]
            scores = jnp.dot(query_half, key_half.T, preferred_element_type=jnp.float32) * factor
            scores = jnp.where(allowed, scores, NEG_BIG)
            row_top = lax.optimization_barrier(jnp.max(scores, axis=1, keepdims=True))
            weights = jnp.where(allowed, jnp.exp(scores - row_top), 0.0)
            row_total = lax.optimization_barrier(jnp.sum(weights, axis=1, keepdims=True))
            summed = jnp.dot(weights.astype(jnp.bfloat16), value_rows, preferred_element_type=jnp.float32)
            results.append(summed / row_total)
        return results[0] - lambdas[head_idx] * results[1]
    heads_out = lax.map(one_head, jnp.arange(HEADS, dtype=jnp.int32))
    attended = jnp.transpose(heads_out, (1, 0, 2))
    mean_sq = lax.optimization_barrier(jnp.mean(attended * attended, axis=-1, keepdims=True))
    normed = (attended * lax.rsqrt(mean_sq + EPSILON) * norm_gain[None] * (1.0 - LAMBDA_INIT)).astype(jnp.bfloat16)
    return jnp.dot(normed.reshape(NQ, HEADS * VW), out_weight, preferred_element_type=jnp.float32).astype(jnp.bfloat16)
```

```python
import functools

import jax
import jax.numpy as jnp
from jax import lax
from jax.experimental import pallas as pl
from jax.experimental.pallas import tpu as pltpu
from jax.sharding import PartitionSpec as P

BLK = 128
NEG_BIG = -1e30
TOP_START = -1e29
LAMBDA_INIT = 0.8
EPSILON = 1e-05
LOG2_E = 1.4426950408889634
MESH = pl.DeviceIdType.MESH
PLANE = 4
RING = 4
PARTS = 4


def attention_kernel(
    q_ref, k_ref, v_ref, low_ref, high_ref, lam_ref, gain_ref, out_ref,
    q_all, k_all, v_all, v_turned, scores, sums, stats, pieces, landed, own_piece, turned_back, normed,
    q1_send, q1_recv, k_send, k_recv, v_send, v_recv, q2_send, q2_recv,
    st_send, st_recv, o_send, o_recv, n_send, n_recv, local_sem,
):
    ctx = lax.axis_index("ctx")
    head = lax.axis_index("head")
    x = ctx // PLANE
    j = lax.rem(ctx, PLANE)
    part_rows = q_all.shape[3]
    tile = PLANE * part_rows
    tokens = k_all.shape[0] * k_all.shape[1]
    value_width = v_all.shape[2]
    half = q_all.shape[4] // 2
    step = min(256, tokens)
    steps = tokens // step
    factor = (half ** -0.5) * LOG2_E
    n_tiles = PARTS * RING

    def plane_device(d):
        return (x * PLANE + lax.rem(j + d, PLANE), head)

    def ring_device(d):
        return (lax.rem(x + d, RING) * PLANE + j, head)

    barrier = pltpu.get_barrier_semaphore()
    for d in range(1, PLANE):
        pl.semaphore_signal(barrier, inc=1, device_id=plane_device(d), device_id_type=MESH)
    for d in range(1, RING):
        pl.semaphore_signal(barrier, inc=1, device_id=ring_device(d), device_id_type=MESH)
    pl.semaphore_wait(barrier, PLANE + RING - 2)

    def q1(d, dst):
        return pltpu.make_async_remote_copy(
            q_ref.at[lax.rem(j + d, PLANE)], q_all.at[:, x, dst], q1_send.at[d], q1_recv.at[d],
            device_id=plane_device(d), device_id_type=MESH)

    def k1(d, dst):
        return pltpu.make_async_remote_copy(
            k_ref.at[lax.rem(j + d, PLANE)], k_all.at[dst], k_send.at[d], k_recv.at[d],
            device_id=plane_device(d), device_id_type=MESH)

    def v1(d, dst):
        return pltpu.make_async_remote_copy(
            v_ref.at[lax.rem(j + d, PLANE)], v_all.at[dst], v_send.at[d], v_recv.at[d],
            device_id=plane_device(d), device_id_type=MESH)

    def q2(r, d, dst):
        return pltpu.make_async_remote_copy(
            q_all.at[r, x], q_all.at[r, dst], q2_send.at[r * RING + d], q2_recv.at[r * RING + d],
            device_id=ring_device(RING - d), device_id_type=MESH)

    def st(r, d, dst):
        return pltpu.make_async_remote_copy(
            stats.at[r, x], stats.at[r, dst], st_send.at[r * RING + d], st_recv.at[r * RING + d],
            device_id=ring_device(RING - d), device_id_type=MESH)

    def o1(r, d, dst):
        return pltpu.make_async_remote_copy(
            pieces.at[r, d], landed.at[r, dst], o_send.at[r * RING + d], o_recv.at[r * RING + d],
            device_id=ring_device(RING - d), device_id_type=MESH)

    def n1(r, d, dst):
        return pltpu.make_async_remote_copy(
            turned_back.at[r, lax.rem(j + d, PLANE)], normed.at[dst, r], n_send.at[r * PLANE + d], n_recv.at[r * PLANE + d],
            device_id=plane_device(d), device_id_type=MESH)

    def plane_source(d):
        return lax.rem(j + PLANE - d, PLANE)

    def ring_source(d):
        return lax.rem(x + d, RING)

    for d in range(1, PLANE):
        q1(d, j).start()
    for d in range(1, PLANE):
        k1(d, j).start()
        v1(d, j).start()
    own_copies = [
        pltpu.make_async_copy(q_ref.at[j], q_all.at[:, x, j], local_sem.at[0]),
        pltpu.make_async_copy(k_ref.at[j], k_all.at[j], local_sem.at[1]),
        pltpu.make_async_copy(v_ref.at[j], v_all.at[j], local_sem.at[2]),
    ]
    for copy in own_copies:
        copy.start()
    own_copies[0].wait()
    for d in range(1, PLANE):
        q1(d, plane_source(d)).wait_recv()
    for r in range(PARTS):
        for d in range(1, RING):
            q2(r, d, x).start()
    own_copies[1].wait()
    own_copies[2].wait()
    for d in range(1, PLANE):
        k1(d, plane_source(d)).wait_recv()
        v1(d, plane_source(d)).wait_recv()
    for source in range(PLANE):
        held = k_all.shape[1]
        v_turned[:, source * held:(source + 1) * held] = v_all[source].T

    def score_step(n, m, t, slot, top):
        r, plane = n // RING, lax.rem(x + lax.rem(n, RING), RING)
        query = q_all[r, plane, :, :, m * half:(m + 1) * half].reshape(tile, half)
        lanes = pl.ds(pl.multiple_of((r * RING + plane) * tile, tile), tile)
        low = low_ref[:, lanes] - x * tokens
        high = high_ref[:, lanes] - x * tokens
        held = k_all.shape[1]
        first = t * step
        if step <= held:
            key = k_all[first // held, first % held:first % held + step, m * half:(m + 1) * half]
        else:
            key = k_all[:, :, m * half:(m + 1) * half].reshape(tokens, half)[first:first + step]
        s = lax.dot_general(key, query, (((1,), (1,)), ((), ())), preferred_element_type=jnp.float32)
        at = lax.broadcasted_iota(jnp.int32, (step, tile), 0) + first
        s = jnp.where((at >= low) & (at < high), s, NEG_BIG)
        scores[slot, first:first + step, :] = s
        return jnp.maximum(top, jnp.max(s, axis=0, keepdims=True))

    def weight_step(t, slot, shift, total, summed):
        first = t * step
        w = jnp.exp2(scores[slot, first:first + step, :] * factor - shift)
        total = total + jnp.sum(w, axis=0, keepdims=True)
        part = jnp.dot(
            v_turned[:, first:first + step], w.astype(jnp.bfloat16), preferred_element_type=jnp.float32)
        return total, (part if summed is None else summed + part)

    def send_stats(r):
        for d in range(1, RING):
            st(r, d, x).start()

    def combine(r):
        for d in range(1, RING):
            st(r, d, ring_source(d)).wait_recv()
        lam = lam_ref[j]
        for d in (1, 3, 2, 0):
            plane = lax.rem(x + RING - d, RING)
            lanes = pl.ds(pl.multiple_of(plane * tile, tile), tile)
            shares = []
            for m in range(2):
                tops = [stats[r, s, 2 * m:2 * m + 1, lanes] for s in range(RING)]
                totals = [stats[r, s, 2 * m + 1:2 * m + 2, lanes] for s in range(RING)]
                top = functools.reduce(jnp.maximum, tops)
                total = sum(a * jnp.exp2((b - top) * factor) for a, b in zip(totals, tops))
                own_top = stats[r, x, 2 * m:2 * m + 1, lanes]
                shares.append(jnp.exp2((own_top - top) * factor) / total)
            piece = sums[r, plane, 0] * shares[0] - sums[r, plane, 1] * (shares[1] * lam)
            if d == 0:
                own_piece[r] = piece
            else:
                pieces[r, d] = piece.astype(jnp.bfloat16)
                o1(r, d, d).start()

    def finish(r):
        for d in range(1, RING):
            o1(r, d, d).wait_recv()
        attended = own_piece[r]
        for d in range(1, RING):
            attended = attended + landed[r, d].astype(jnp.float32)
        mean_sq = jnp.mean(attended * attended, axis=0, keepdims=True)
        result = attended * lax.rsqrt(mean_sq + EPSILON)
        result = result * gain_ref[j, :, 0:1] * (1.0 - LAMBDA_INIT)
        turned_back[r] = result.T.astype(jnp.bfloat16).reshape(PLANE, part_rows, value_width)
        for d in range(1, PLANE):
            n1(r, d, j).start()
        normed[j, r] = turned_back[r, j]

    first_top = jnp.full((1, tile), TOP_START, jnp.float32)
    top = first_top
    for t in range(steps):
        top = score_step(0, 0, t, 0, top)

    def body(n, top):
        r, d = n // RING, lax.rem(n, RING)
        plane = lax.rem(x + d, RING)
        later = jnp.minimum(n + 1, n_tiles - 1)
        later_r, later_d = later // RING, lax.rem(later, RING)

        @pl.when((n + 1 < n_tiles) & (later_d > 0))
        def _():
            q2(later_r, later_d, ring_source(later_d)).wait_recv()

        lanes = pl.ds(pl.multiple_of(plane * tile, tile), tile)
        for m in range(2):
            next_top = first_top
            total = jnp.zeros((1, tile), jnp.float32)
            summed = None
            shift = top * factor
            for t in range(steps):
                next_top = score_step(n if m == 0 else later, 1 - m, t, 1 - m, next_top)
                total, summed = weight_step(t, m, shift, total, summed)
            sums[r, plane, m] = summed
            stats[r, x, 2 * m:2 * m + 1, lanes] = top
            stats[r, x, 2 * m + 1:2 * m + 2, lanes] = total
            top = next_top

        @pl.when(d == RING - 1)
        def _():
            send_stats(r)

        @pl.when((d == 1) & (n >= RING))
        def _():
            combine(r - 1)

        @pl.when((d == 2) & (n >= 2 * RING))
        def _():
            finish(r - 2)

        return top

    lax.fori_loop(0, n_tiles, body, top)
    combine(PARTS - 1)
    finish(PARTS - 2)
    finish(PARTS - 1)

    def last_waits(r, carry):
        for d in range(1, PLANE):
            n1(r, d, plane_source(d)).wait_recv()
            n1(r, d, j).wait_send()
        for d in range(1, RING):
            q2(r, d, x).wait_send()
            st(r, d, x).wait_send()
            o1(r, d, d).wait_send()
        return carry

    lax.fori_loop(0, PARTS, last_waits, 0)
    for d in range(1, PLANE):
        q1(d, j).wait_send()
        k1(d, j).wait_send()
        v1(d, j).wait_send()
    for source in range(PLANE):
        out_ref[:, source * value_width:(source + 1) * value_width] = normed[source].reshape(
            PARTS * part_rows, value_width)


def attention(queries, keys, values, low, high, lambdas, gain):
    heads, parts, part_rows, width = queries.shape
    held, value_width = values.shape[1:]
    tile = PLANE * part_rows
    tokens = PLANE * held
    vmem = pl.BlockSpec(memory_space=pltpu.VMEM)
    hbm = pl.BlockSpec(memory_space=pl.ANY)
    bf16, f32 = jnp.bfloat16, jnp.float32
    dma = pltpu.SemaphoreType.DMA
    return pl.pallas_call(
        attention_kernel,
        out_shape=jax.ShapeDtypeStruct((parts * part_rows, heads * value_width), bf16),
        in_specs=[hbm, hbm, hbm, vmem, vmem, pl.BlockSpec(memory_space=pltpu.SMEM), vmem],
        out_specs=vmem,
        scratch_shapes=[
            pltpu.VMEM((PARTS, RING, PLANE, part_rows, width), bf16),
            pltpu.VMEM((PLANE, held, width), bf16),
            pltpu.VMEM((PLANE, held, value_width), bf16),
            pltpu.VMEM((value_width, tokens), bf16),
            pltpu.VMEM((2, tokens, tile), f32),
            pltpu.VMEM((PARTS, RING, 2, value_width, tile), f32),
            pltpu.VMEM((PARTS, RING, 8, RING * tile), f32),
            pltpu.VMEM((PARTS, RING, value_width, tile), bf16),
            pltpu.VMEM((PARTS, RING, value_width, tile), bf16),
            pltpu.VMEM((PARTS, value_width, tile), f32),
            pltpu.VMEM((PARTS, PLANE, part_rows, value_width), bf16),
            pltpu.VMEM((PLANE, PARTS, part_rows, value_width), bf16),
            dma((PLANE,)), dma((PLANE,)), dma((PLANE,)), dma((PLANE,)), dma((PLANE,)), dma((PLANE,)),
            dma((PARTS * RING,)), dma((PARTS * RING,)), dma((PARTS * RING,)), dma((PARTS * RING,)),
            dma((PARTS * RING,)), dma((PARTS * RING,)), dma((PARTS * PLANE,)), dma((PARTS * PLANE,)),
            dma((3,)),
        ],
        compiler_params=pltpu.CompilerParams(
            collective_id=0, has_side_effects=True, vmem_limit_bytes=56 * 1024 * 1024),
    )(queries, keys, values, low, high, lambdas, gain)


def per_device(
    queries, cache_keys, cache_values, positions, doc_spans, lambdas, norm_gain, out_weight
):
    q_rows, heads_here, both_width = queries.shape
    part_rows = q_rows // PARTS
    by_head = lambda a: jnp.transpose(a, (1, 0, 2))
    asked = by_head(queries).reshape(heads_here, PARTS, part_rows, both_width)
    ordered = lambda a: a.reshape(RING, PLANE, PARTS, part_rows).transpose(2, 0, 1, 3).reshape(1, -1)
    low = ordered(doc_spans[:, 0] * BLK)
    high = ordered(jnp.minimum(positions + 1, doc_spans[:, 1] * BLK))
    gain = jnp.broadcast_to(norm_gain[:, :, None], norm_gain.shape + (128,))
    flat_rows = attention(
        asked, by_head(cache_keys), by_head(cache_values), low, high, lambdas, gain)
    return lax.psum_scatter(
        jnp.dot(flat_rows, out_weight, preferred_element_type=jnp.float32).astype(jnp.bfloat16),
        "head",
        scatter_dimension=0,
        tiled=True,
    )


def solution(mesh):
    placed = (
        P("ctx", "head", None),
        P("ctx", "head", None),
        P("ctx", "head", None),
        P(),
        P(),
        P("head"),
        P("head", None),
        P("head", None),
    )
    return jax.shard_map(
        per_device, mesh=mesh, in_specs=placed, out_specs=P(("ctx", "head"), None), check_vma=False
    )
```

```python
import functools

import jax
import jax.numpy as jnp
from jax import lax
from jax.experimental import pallas as pl
from jax.experimental.pallas import tpu as pltpu
from jax.sharding import PartitionSpec as P

BLK = 128
NEG_BIG = -1e30
TOP_START = -1e29
LAMBDA_INIT = 0.8
EPSILON = 1e-05
LOG2_E = 1.4426950408889634
MESH = pl.DeviceIdType.MESH
PLANE = 4
RING = 4
COLUMN = 4
SIDES = 2
WEIGHTS_AT = 10
PARTS = 4


def attention_kernel(
    q_ref, k_ref, v_ref, low_ref, high_ref, lam_ref, gain_ref, w_ref, out_ref,
    q_all, k_all, v_all, v_turned, scores, sums, stats, pieces, landed, own_piece, turned_back, normed,
    w_all, a_out, a_in, b_out, b_in, a_mine, a2_out, a2_in, b2_out, b2_in, result,
    q1_send, q1_recv, k_send, k_recv, v_send, v_recv, q2_send, q2_recv,
    st_send, st_recv, o_send, o_recv, n_send, n_recv, local_sem,
    a_send, a_recv, b_send, b_recv, a2_send, a2_recv, b2_send, b2_recv,
):
    ctx = lax.axis_index("ctx")
    head = lax.axis_index("head")
    x = ctx // PLANE
    j = lax.rem(ctx, PLANE)
    y = head // SIDES
    side = lax.rem(head, SIDES)
    part_rows = q_all.shape[3]
    tile = PLANE * part_rows
    tokens = k_all.shape[0] * k_all.shape[1]
    value_width = v_all.shape[2]
    half = q_all.shape[4] // 2
    step = min(256, tokens)
    steps = tokens // step
    factor = (half ** -0.5) * LOG2_E
    n_tiles = PARTS * RING
    share = part_rows // (COLUMN * SIDES)
    columns = w_ref.shape[1]
    area = columns // 2
    fold = area // 2
    stripe = min(512, fold)

    def plane_device(d):
        return (x * PLANE + lax.rem(j + d, PLANE), head)

    def ring_device(d):
        return (lax.rem(x + d, RING) * PLANE + j, head)

    def column_device(d):
        return (ctx, lax.rem(y + d, COLUMN) * SIDES + side)

    other_side = (ctx, y * SIDES + 1 - side)

    barrier = pltpu.get_barrier_semaphore()
    for d in range(1, PLANE):
        pl.semaphore_signal(barrier, inc=1, device_id=plane_device(d), device_id_type=MESH)
    for d in range(1, RING):
        pl.semaphore_signal(barrier, inc=1, device_id=ring_device(d), device_id_type=MESH)
    for d in range(1, COLUMN):
        pl.semaphore_signal(barrier, inc=1, device_id=column_device(d), device_id_type=MESH)
    pl.semaphore_signal(barrier, inc=1, device_id=other_side, device_id_type=MESH)
    pl.semaphore_wait(barrier, PLANE + RING + COLUMN - 2)

    def q1(d, dst):
        return pltpu.make_async_remote_copy(
            q_ref.at[lax.rem(j + d, PLANE)], q_all.at[:, x, dst], q1_send.at[d], q1_recv.at[d],
            device_id=plane_device(d), device_id_type=MESH)

    def k1(d, dst):
        return pltpu.make_async_remote_copy(
            k_ref.at[lax.rem(j + d, PLANE)], k_all.at[dst], k_send.at[d], k_recv.at[d],
            device_id=plane_device(d), device_id_type=MESH)

    def v1(d, dst):
        return pltpu.make_async_remote_copy(
            v_ref.at[lax.rem(j + d, PLANE)], v_all.at[dst], v_send.at[d], v_recv.at[d],
            device_id=plane_device(d), device_id_type=MESH)

    def q2(r, d, dst):
        return pltpu.make_async_remote_copy(
            q_all.at[r, x], q_all.at[r, dst], q2_send.at[r * RING + d], q2_recv.at[r * RING + d],
            device_id=ring_device(RING - d), device_id_type=MESH)

    def st(r, d, dst):
        return pltpu.make_async_remote_copy(
            stats.at[r, x], stats.at[r, dst], st_send.at[r * RING + d], st_recv.at[r * RING + d],
            device_id=ring_device(RING - d), device_id_type=MESH)

    def o1(r, d, dst):
        return pltpu.make_async_remote_copy(
            pieces.at[r, d], landed.at[r, dst], o_send.at[r * RING + d], o_recv.at[r * RING + d],
            device_id=ring_device(RING - d), device_id_type=MESH)

    def n1(r, d, dst):
        return pltpu.make_async_remote_copy(
            turned_back.at[r, lax.rem(j + d, PLANE)], normed.at[dst, r], n_send.at[r * PLANE + d], n_recv.at[r * PLANE + d],
            device_id=plane_device(d), device_id_type=MESH)

    def a1(r, d):
        return pltpu.make_async_remote_copy(
            a_out.at[r, lax.rem(y + d, COLUMN)], a_in.at[r, d], a_send.at[r * COLUMN + d], a_recv.at[r * COLUMN + d],
            device_id=column_device(d), device_id_type=MESH)

    def a2(r):
        return pltpu.make_async_remote_copy(
            a2_out.at[r], a2_in.at[r], a2_send.at[r], a2_recv.at[r], device_id=other_side, device_id_type=MESH)

    def b1(r):
        return pltpu.make_async_remote_copy(
            b_out.at[r, 1 - side], b_in.at[r], b_send.at[r], b_recv.at[r], device_id=other_side, device_id_type=MESH)

    def b2(r, d):
        return pltpu.make_async_remote_copy(
            b2_out.at[r, lax.rem(y + d, COLUMN)], b2_in.at[r, d], b2_send.at[r * COLUMN + d], b2_recv.at[r * COLUMN + d],
            device_id=column_device(d), device_id_type=MESH)

    def plane_source(d):
        return lax.rem(j + PLANE - d, PLANE)

    def ring_source(d):
        return lax.rem(x + d, RING)

    for d in range(1, PLANE):
        q1(d, j).start()
    for d in range(1, PLANE):
        k1(d, j).start()
        v1(d, j).start()
    own_copies = [
        pltpu.make_async_copy(q_ref.at[j], q_all.at[:, x, j], local_sem.at[0]),
        pltpu.make_async_copy(k_ref.at[j], k_all.at[j], local_sem.at[1]),
        pltpu.make_async_copy(v_ref.at[j], v_all.at[j], local_sem.at[2]),
    ]
    for copy in own_copies:
        copy.start()
    weights_copy = pltpu.make_async_copy(w_ref, w_all, local_sem.at[3])
    weights_copy.start()
    own_copies[0].wait()
    for d in range(1, PLANE):
        q1(d, plane_source(d)).wait_recv()
    for r in range(PARTS):
        for d in range(1, RING):
            q2(r, d, x).start()
    own_copies[1].wait()
    own_copies[2].wait()
    for d in range(1, PLANE):
        k1(d, plane_source(d)).wait_recv()
        v1(d, plane_source(d)).wait_recv()
    for source in range(PLANE):
        held = k_all.shape[1]
        v_turned[:, source * held:(source + 1) * held] = v_all[source].T

    def score_step(n, m, t, slot, top):
        r, plane = n // RING, lax.rem(x + lax.rem(n, RING), RING)
        query = q_all[r, plane, :, :, m * half:(m + 1) * half].reshape(tile, half)
        lanes = pl.ds(pl.multiple_of((r * RING + plane) * tile, tile), tile)
        low = low_ref[:, lanes] - x * tokens
        high = high_ref[:, lanes] - x * tokens
        held = k_all.shape[1]
        first = t * step
        if step <= held:
            key = k_all[first // held, first % held:first % held + step, m * half:(m + 1) * half]
        else:
            key = k_all[:, :, m * half:(m + 1) * half].reshape(tokens, half)[first:first + step]
        s = lax.dot_general(key, query, (((1,), (1,)), ((), ())), preferred_element_type=jnp.float32)
        at = lax.broadcasted_iota(jnp.int32, (step, tile), 0) + first
        s = jnp.where((at >= low) & (at < high), s, NEG_BIG)
        scores[slot, first:first + step, :] = s
        return jnp.maximum(top, jnp.max(s, axis=0, keepdims=True))

    def weight_step(t, slot, shift, total, summed):
        first = t * step
        w = jnp.exp2(scores[slot, first:first + step, :] * factor - shift)
        total = total + jnp.sum(w, axis=0, keepdims=True)
        part = jnp.dot(
            v_turned[:, first:first + step], w.astype(jnp.bfloat16), preferred_element_type=jnp.float32)
        return total, (part if summed is None else summed + part)

    def send_stats(r):
        for d in range(1, RING):
            st(r, d, x).start()

    def combine(r):
        for d in range(1, RING):
            st(r, d, ring_source(d)).wait_recv()
        lam = lam_ref[j]
        for d in (1, 3, 2, 0):
            plane = lax.rem(x + RING - d, RING)
            lanes = pl.ds(pl.multiple_of(plane * tile, tile), tile)
            shares = []
            for m in range(2):
                tops = [stats[r, s, 2 * m:2 * m + 1, lanes] for s in range(RING)]
                totals = [stats[r, s, 2 * m + 1:2 * m + 2, lanes] for s in range(RING)]
                top = functools.reduce(jnp.maximum, tops)
                total = sum(a * jnp.exp2((b - top) * factor) for a, b in zip(totals, tops))
                own_top = stats[r, x, 2 * m:2 * m + 1, lanes]
                shares.append(jnp.exp2((own_top - top) * factor) / total)
            piece = sums[r, plane, 0] * shares[0] - sums[r, plane, 1] * (shares[1] * lam)
            if d == 0:
                own_piece[r] = piece
            else:
                pieces[r, d] = piece.astype(jnp.bfloat16)
                o1(r, d, d).start()

    def finish(r):
        for d in range(1, RING):
            o1(r, d, d).wait_recv()
        attended = own_piece[r]
        for d in range(1, RING):
            attended = attended + landed[r, d].astype(jnp.float32)
        mean_sq = jnp.mean(attended * attended, axis=0, keepdims=True)
        result = attended * lax.rsqrt(mean_sq + EPSILON)
        result = result * gain_ref[j, :, 0:1] * (1.0 - LAMBDA_INIT)
        turned_back[r] = result.T.astype(jnp.bfloat16).reshape(PLANE, part_rows, value_width)
        for d in range(1, PLANE):
            n1(r, d, j).start()
        normed[j, r] = turned_back[r, j]

    def project(r):
        for d in range(1, PLANE):
            n1(r, d, plane_source(d)).wait_recv()
        rows = jnp.concatenate([normed[h, r] for h in range(PLANE)], axis=1)

        def product(first):
            return jnp.dot(rows, w_all[:, pl.ds(pl.multiple_of(first, stripe), stripe)], preferred_element_type=jnp.float32)

        def b_stripe(i, carry):
            at = pl.ds(pl.multiple_of(i * stripe, stripe), stripe)
            got = product(area + i * stripe).astype(jnp.bfloat16)
            for side_to in range(SIDES):
                b_out[r, side_to, :, at] = got[side_to * COLUMN * share:(side_to + 1) * COLUMN * share]
            return carry

        def a_stripe(i, carry):
            at = pl.ds(pl.multiple_of(i * stripe, stripe), stripe)
            got = product(i * stripe)
            for y_to in range(COLUMN):
                a_out[r, y_to, :, at] = jnp.concatenate(
                    [got[(s * COLUMN + y_to) * share:(s * COLUMN + y_to + 1) * share] for s in range(SIDES)], axis=0
                ).astype(jnp.bfloat16)
            return carry

        lax.fori_loop(0, area // stripe, b_stripe, 0)
        b1(r).start()
        lax.fori_loop(0, area // stripe, a_stripe, 0)
        for d in (1, 3, 2):
            a1(r, d).start()

    def add_first(r):
        b1(r).wait_recv()

        def b_stripe(i, carry):
            halves = []
            for k in range(2):
                at = pl.ds(pl.multiple_of(k * fold + i * stripe, stripe), stripe)
                halves.append(b_out[r, side, :, at].astype(jnp.float32) + b_in[r, :, at].astype(jnp.float32))
            at = pl.ds(pl.multiple_of(i * stripe, stripe), stripe)
            for y_to in range(COLUMN):
                b2_out[r, y_to, :, at] = jnp.concatenate(
                    [got[y_to * share:(y_to + 1) * share] for got in halves], axis=0).astype(jnp.bfloat16)
            return carry

        lax.fori_loop(0, fold // stripe, b_stripe, 0)
        for d in (1, 3, 2):
            b2(r, d).start()
        for d in range(1, COLUMN):
            a1(r, d).wait_recv()

        def a_stripe(i, carry):
            others = []
            for k in range(2):
                at = pl.ds(pl.multiple_of(k * fold + i * stripe, stripe), stripe)
                got = a_out[r, y, :, at].astype(jnp.float32)
                for d in range(1, COLUMN):
                    got = got + a_in[r, d, :, at].astype(jnp.float32)
                a_mine[r, :, at] = jnp.where(side == 0, got[:share], got[share:])
                others.append(jnp.where(side == 0, got[share:], got[:share]))
            at = pl.ds(pl.multiple_of(i * stripe, stripe), stripe)
            a2_out[r, :, at] = jnp.concatenate(others, axis=0).astype(jnp.bfloat16)
            return carry

        lax.fori_loop(0, fold // stripe, a_stripe, 0)
        a2(r).start()

    def add_last(r):
        for d in range(1, COLUMN):
            b2(r, d).wait_recv()
        a2(r).wait_recv()

        def last_stripe(i, carry):
            at = pl.ds(pl.multiple_of(i * stripe, stripe), stripe)
            a_got = a2_in[r, :, at].astype(jnp.float32)
            b_got = b2_out[r, y, :, at].astype(jnp.float32)
            for d in range(1, COLUMN):
                b_got = b_got + b2_in[r, d, :, at].astype(jnp.float32)
            for k in range(2):
                rows = slice(k * share, (k + 1) * share)
                here = pl.ds(pl.multiple_of(k * fold + i * stripe, stripe), stripe)
                result[r, :, here] = a_mine[r, :, here] + a_got[rows]
                there = pl.ds(pl.multiple_of(area + k * fold + i * stripe, stripe), stripe)
                result[r, :, there] = b_got[rows]
            return carry

        lax.fori_loop(0, fold // stripe, last_stripe, 0)

    stages = ((send_stats, 3), (combine, 5), (finish, 10), (project, 12), (add_first, 17), (add_last, 20))

    def run_stages(n):
        for stage, lag in reversed(stages):
            @pl.when((n >= lag) & (n < lag + PARTS * RING) & (lax.rem(n + RING * RING - lag, RING) == 0))
            def _():
                stage((n - lag) // RING)

    first_top = jnp.full((1, tile), TOP_START, jnp.float32)
    top = first_top
    for t in range(steps):
        top = score_step(0, 0, t, 0, top)

    def body(n, top):
        r, d = n // RING, lax.rem(n, RING)
        plane = lax.rem(x + d, RING)
        later = jnp.minimum(n + 1, n_tiles - 1)
        later_r, later_d = later // RING, lax.rem(later, RING)

        @pl.when((n + 1 < n_tiles) & (later_d > 0))
        def _():
            q2(later_r, later_d, ring_source(later_d)).wait_recv()

        lanes = pl.ds(pl.multiple_of(plane * tile, tile), tile)
        for m in range(2):
            next_top = first_top
            total = jnp.zeros((1, tile), jnp.float32)
            summed = None
            shift = top * factor
            for t in range(steps):
                next_top = score_step(n if m == 0 else later, 1 - m, t, 1 - m, next_top)
                total, summed = weight_step(t, m, shift, total, summed)
            sums[r, plane, m] = summed
            stats[r, x, 2 * m:2 * m + 1, lanes] = top
            stats[r, x, 2 * m + 1:2 * m + 2, lanes] = total
            top = next_top

        @pl.when(n == WEIGHTS_AT)
        def _():
            weights_copy.wait()

        run_stages(n)
        return top

    lax.fori_loop(0, n_tiles, body, top)

    def tail(n, carry):
        run_stages(n)
        return carry

    lax.fori_loop(n_tiles, n_tiles - RING + stages[-1][1] + 1, tail, 0)

    def last_waits(r, carry):
        for d in range(1, PLANE):
            n1(r, d, j).wait_send()
        for d in range(1, RING):
            q2(r, d, x).wait_send()
            st(r, d, x).wait_send()
            o1(r, d, d).wait_send()
        for d in range(1, COLUMN):
            a1(r, d).wait_send()
            b2(r, d).wait_send()
        a2(r).wait_send()
        b1(r).wait_send()
        return carry

    lax.fori_loop(0, PARTS, last_waits, 0)
    for d in range(1, PLANE):
        q1(d, j).wait_send()
        k1(d, j).wait_send()
        v1(d, j).wait_send()
    for i in range(columns // stripe):
        at = slice(i * stripe, (i + 1) * stripe)
        out_ref[:, at] = jnp.concatenate([result[r, :, at] for r in range(PARTS)], axis=0).astype(jnp.bfloat16)


def layer(queries, keys, values, low, high, lambdas, gain, weights):
    heads, parts, part_rows, width = queries.shape
    held, value_width = values.shape[1:]
    tile = PLANE * part_rows
    tokens = PLANE * held
    vmem = pl.BlockSpec(memory_space=pltpu.VMEM)
    hbm = pl.BlockSpec(memory_space=pl.ANY)
    bf16, f32 = jnp.bfloat16, jnp.float32
    share = part_rows // (COLUMN * SIDES)
    columns = weights.shape[1]
    area = columns // 2
    dma = pltpu.SemaphoreType.DMA
    return pl.pallas_call(
        attention_kernel,
        out_shape=jax.ShapeDtypeStruct((parts * share, columns), bf16),
        in_specs=[hbm, hbm, hbm, vmem, vmem, pl.BlockSpec(memory_space=pltpu.SMEM), vmem, hbm],
        out_specs=vmem,
        scratch_shapes=[
            pltpu.VMEM((PARTS, RING, PLANE, part_rows, width), bf16),
            pltpu.VMEM((PLANE, held, width), bf16),
            pltpu.VMEM((PLANE, held, value_width), bf16),
            pltpu.VMEM((value_width, tokens), bf16),
            pltpu.VMEM((2, tokens, tile), f32),
            pltpu.VMEM((PARTS, RING, 2, value_width, tile), f32),
            pltpu.VMEM((PARTS, RING, 8, RING * tile), f32),
            pltpu.VMEM((PARTS, RING, value_width, tile), bf16),
            pltpu.VMEM((PARTS, RING, value_width, tile), bf16),
            pltpu.VMEM((PARTS, value_width, tile), f32),
            pltpu.VMEM((PARTS, PLANE, part_rows, value_width), bf16),
            pltpu.VMEM((PLANE, PARTS, part_rows, value_width), bf16),
            pltpu.VMEM(weights.shape, bf16),
            pltpu.VMEM((PARTS, COLUMN, SIDES * share, area), bf16),
            pltpu.VMEM((PARTS, COLUMN, SIDES * share, area), bf16),
            pltpu.VMEM((PARTS, SIDES, COLUMN * share, area), bf16),
            pltpu.VMEM((PARTS, COLUMN * share, area), bf16),
            pltpu.VMEM((PARTS, share, area), f32),
            pltpu.VMEM((PARTS, 2 * share, area // 2), bf16),
            pltpu.VMEM((PARTS, 2 * share, area // 2), bf16),
            pltpu.VMEM((PARTS, COLUMN, 2 * share, area // 2), bf16),
            pltpu.VMEM((PARTS, COLUMN, 2 * share, area // 2), bf16),
            pltpu.VMEM((PARTS, share, columns), f32),
            dma((PLANE,)), dma((PLANE,)), dma((PLANE,)), dma((PLANE,)), dma((PLANE,)), dma((PLANE,)),
            dma((PARTS * RING,)), dma((PARTS * RING,)), dma((PARTS * RING,)), dma((PARTS * RING,)),
            dma((PARTS * RING,)), dma((PARTS * RING,)), dma((PARTS * PLANE,)), dma((PARTS * PLANE,)),
            dma((4,)),
            dma((PARTS * COLUMN,)), dma((PARTS * COLUMN,)), dma((PARTS,)), dma((PARTS,)),
            dma((PARTS,)), dma((PARTS,)), dma((PARTS * COLUMN,)), dma((PARTS * COLUMN,)),
        ],
        compiler_params=pltpu.CompilerParams(
            collective_id=0, has_side_effects=True, vmem_limit_bytes=60 * 1024 * 1024),
    )(queries, keys, values, low, high, lambdas, gain, weights)


def per_device(
    queries, cache_keys, cache_values, positions, doc_spans, lambdas, norm_gain, out_weight
):
    q_rows, heads_here, both_width = queries.shape
    part_rows = q_rows // PARTS
    share = part_rows // (COLUMN * SIDES)
    by_head = lambda a: jnp.transpose(a, (1, 0, 2))
    asked = queries.reshape(COLUMN, SIDES, PARTS, share, heads_here, both_width).transpose(4, 2, 1, 0, 3, 5)
    asked = asked.reshape(heads_here, PARTS, part_rows, both_width)
    ordered = lambda a: a.reshape(RING, PLANE, COLUMN, SIDES, PARTS, share).transpose(4, 0, 1, 3, 2, 5).reshape(1, -1)
    low = ordered(doc_spans[:, 0] * BLK)
    high = ordered(jnp.minimum(positions + 1, doc_spans[:, 1] * BLK))
    gain = jnp.broadcast_to(norm_gain[:, :, None], norm_gain.shape + (128,))
    return layer(
        asked, by_head(cache_keys), by_head(cache_values), low, high, lambdas, gain, out_weight)


def solution(mesh):
    placed = (
        P("ctx", "head", None),
        P("ctx", "head", None),
        P("ctx", "head", None),
        P(),
        P(),
        P("head"),
        P("head", None),
        P("head", None),
    )
    return jax.shard_map(
        per_device, mesh=mesh, in_specs=placed, out_specs=P(("ctx", "head"), None), check_vma=False
    )
```

```python
import functools

import jax
import jax.numpy as jnp
from jax import lax
from jax.experimental import pallas as pl
from jax.experimental.pallas import tpu as pltpu
from jax.sharding import PartitionSpec as P

BLK = 128
NEG_BIG = -1e30
TOP_START = -1e29
LAMBDA_INIT = 0.8
EPSILON = 1e-05
LOG2_E = 1.4426950408889634
MESH = pl.DeviceIdType.MESH
PLANE = 4
RING = 4
COLUMN = 4
SIDES = 2
HALVES = 2
PARTS = 4


def attention_kernel(
    q_ref, k_ref, v_ref, span_ref, lam_ref, gain_ref, w_ref, out_ref,
    q_all, k_all, v_all, v_turned, scores, sums, stats, pieces, landed, own_piece, turned_back, normed,
    w_all, a_out, a_in, b_out, b_in, a_mine, a2_out, a2_in, b2_out, b2_in, result,
    q1_send, q1_recv, k_send, k_recv, v_send, v_recv, q2_send, q2_recv,
    st_send, st_recv, o_send, o_recv, n_send, n_recv, local_sem,
    a_send, a_recv, b_send, b_recv, a2_send, a2_recv, b2_send, b2_recv,
):
    ctx = lax.axis_index("ctx")
    head = lax.axis_index("head")
    x = ctx // PLANE
    j = lax.rem(ctx, PLANE)
    y = head // SIDES
    side = lax.rem(head, SIDES)
    part_rows = q_all.shape[3]
    tile = PLANE * part_rows
    held = k_all.shape[1]
    tokens = PLANE * held
    near = tokens // HALVES
    value_width = v_all.shape[2]
    half = q_all.shape[4] // 2
    step = min(256, held)
    steps = near // step
    factor = (half ** -0.5) * LOG2_E
    half_tiles = PARTS * RING
    n_tiles = HALVES * half_tiles
    zp = j // 2
    core = lax.rem(j, 2)
    share = part_rows // (COLUMN * SIDES)
    columns = w_ref.shape[1]
    area = columns // 2
    fold = area // 2
    stripe = min(512, fold)

    def partner(k):
        return (2 * zp + 1 - core, 2 * (1 - zp) + core, PLANE - 1 - j)[k - 1]

    def plane_device(k):
        return (x * PLANE + partner(k), head)

    def ring_device(d):
        return (lax.rem(x + d, RING) * PLANE + j, head)

    def column_device(d):
        return (ctx, lax.rem(y + d, COLUMN) * SIDES + side)

    other_side = (ctx, y * SIDES + 1 - side)

    barrier = pltpu.get_barrier_semaphore()
    for d in range(1, PLANE):
        pl.semaphore_signal(barrier, inc=1, device_id=plane_device(d), device_id_type=MESH)
    for d in range(1, RING):
        pl.semaphore_signal(barrier, inc=1, device_id=ring_device(d), device_id_type=MESH)
    for d in range(1, COLUMN):
        pl.semaphore_signal(barrier, inc=1, device_id=column_device(d), device_id_type=MESH)
    pl.semaphore_signal(barrier, inc=1, device_id=other_side, device_id_type=MESH)
    pl.semaphore_wait(barrier, PLANE + RING + COLUMN - 2)

    def q1(d, dst):
        return pltpu.make_async_remote_copy(
            q_ref.at[partner(d)], q_all.at[:, x, dst], q1_send.at[d], q1_recv.at[d],
            device_id=plane_device(d), device_id_type=MESH)

    def k1(d, dst):
        return pltpu.make_async_remote_copy(
            k_ref.at[partner(d)], k_all.at[dst], k_send.at[d], k_recv.at[d],
            device_id=plane_device(d), device_id_type=MESH)

    def v1(d, dst):
        return pltpu.make_async_remote_copy(
            v_ref.at[partner(d)], v_all.at[dst], v_send.at[d], v_recv.at[d],
            device_id=plane_device(d), device_id_type=MESH)

    def q2(r, d, dst):
        return pltpu.make_async_remote_copy(
            q_all.at[r, x], q_all.at[r, dst], q2_send.at[r * RING + d], q2_recv.at[r * RING + d],
            device_id=ring_device(RING - d), device_id_type=MESH)

    def st(r, d, dst):
        return pltpu.make_async_remote_copy(
            stats.at[r, x], stats.at[r, dst], st_send.at[r * RING + d], st_recv.at[r * RING + d],
            device_id=ring_device(RING - d), device_id_type=MESH)

    def o1(r, d, dst):
        return pltpu.make_async_remote_copy(
            pieces.at[r, d], landed.at[r, dst], o_send.at[r * RING + d], o_recv.at[r * RING + d],
            device_id=ring_device(RING - d), device_id_type=MESH)

    def n1(r, d, dst):
        return pltpu.make_async_remote_copy(
            turned_back.at[r, partner(d)], normed.at[dst, r], n_send.at[r * PLANE + d], n_recv.at[r * PLANE + d],
            device_id=plane_device(d), device_id_type=MESH)

    def a1(r, d):
        return pltpu.make_async_remote_copy(
            a_out.at[r, lax.rem(y + d, COLUMN)], a_in.at[r, d], a_send.at[r * COLUMN + d], a_recv.at[r * COLUMN + d],
            device_id=column_device(d), device_id_type=MESH)

    def a2(r):
        return pltpu.make_async_remote_copy(
            a2_out.at[r], a2_in.at[r], a2_send.at[r], a2_recv.at[r], device_id=other_side, device_id_type=MESH)

    def b1(r):
        return pltpu.make_async_remote_copy(
            b_out.at[r, 1 - side], b_in.at[r], b_send.at[r], b_recv.at[r], device_id=other_side, device_id_type=MESH)

    def b2(r, d):
        return pltpu.make_async_remote_copy(
            b2_out.at[r, lax.rem(y + d, COLUMN)], b2_in.at[r, d], b2_send.at[r * COLUMN + d], b2_recv.at[r * COLUMN + d],
            device_id=column_device(d), device_id_type=MESH)

    def ring_source(d):
        return lax.rem(x + d, RING)

    for d in range(1, PLANE):
        q1(d, j).start()
    for d in range(1, PLANE):
        k1(d, j).start()
        v1(d, j).start()
    own_copies = [
        pltpu.make_async_copy(q_ref.at[j], q_all.at[:, x, j], local_sem.at[0]),
        pltpu.make_async_copy(k_ref.at[j], k_all.at[j], local_sem.at[1]),
        pltpu.make_async_copy(v_ref.at[j], v_all.at[j], local_sem.at[2]),
    ]
    for copy in own_copies:
        copy.start()
    weights_copy = pltpu.make_async_copy(w_ref, w_all, local_sem.at[3])
    weights_copy.start()
    def clear(i, carry):
        r, plane = i // RING, lax.rem(i, RING)
        sums[r, plane] = jnp.zeros(sums.shape[2:], jnp.float32)
        lanes = pl.ds(pl.multiple_of(plane * tile, tile), tile)
        for m in range(2):
            stats[r, x, 2 * m:2 * m + 1, lanes] = jnp.full((1, tile), TOP_START, jnp.float32)
            stats[r, x, 2 * m + 1:2 * m + 2, lanes] = jnp.zeros((1, tile), jnp.float32)
        return carry

    lax.fori_loop(0, half_tiles, clear, 0)
    own_copies[0].wait()
    for d in range(1, PLANE):
        q1(d, partner(d)).wait_recv()
    for r in range(PARTS):
        for d in (1, 3, 2):
            q2(r, d, x).start()
    own_copies[1].wait()
    own_copies[2].wait()
    k1(1, partner(1)).wait_recv()
    v1(1, partner(1)).wait_recv()
    for source in (j, partner(1)):
        v_turned[source] = v_all[source].T

    def place(n):
        late = n // half_tiles
        at = lax.rem(n, half_tiles)
        return 2 * (zp + late - 2 * zp * late), at // RING, lax.rem(x + lax.rem(at, RING), RING)

    def score_step(n, m, t, slot, top):
        source, r, plane = place(n)
        query = q_all[r, plane, :, :, m * half:(m + 1) * half].reshape(tile, half)
        lanes = pl.ds(pl.multiple_of((r * RING + plane) * tile, tile), tile)
        base = x * tokens + source * held
        low = span_ref[0:1, lanes] - base
        high = span_ref[1:2, lanes] - base
        first = t * step
        key = k_all[source + first // held, first % held:first % held + step, m * half:(m + 1) * half]
        s = lax.dot_general(key, query, (((1,), (1,)), ((), ())), preferred_element_type=jnp.float32)
        at = lax.broadcasted_iota(jnp.int32, (step, tile), 0) + first
        s = jnp.where((at >= low) & (at < high), s, NEG_BIG)
        scores[slot, first:first + step, :] = s
        return jnp.maximum(top, jnp.max(s, axis=0, keepdims=True))

    def weight_step(n, t, slot, shift, total, summed):
        source, _, _ = place(n)
        first = t * step
        w = jnp.exp2(scores[slot, first:first + step, :] * factor - shift)
        total = total + jnp.sum(w, axis=0, keepdims=True)
        part = jnp.dot(
            v_turned[source + first // held, :, first % held:first % held + step], w.astype(jnp.bfloat16),
            preferred_element_type=jnp.float32)
        return total, (part if summed is None else summed + part)

    def send_stats(r):
        for d in range(1, RING):
            st(r, d, x).start()

    def combine(r):
        for d in range(1, RING):
            st(r, d, ring_source(d)).wait_recv()
        lam = lam_ref[j]
        for d in (1, 3, 2, 0):
            plane = lax.rem(x + RING - d, RING)
            lanes = pl.ds(pl.multiple_of(plane * tile, tile), tile)
            shares = []
            for m in range(2):
                tops = [stats[r, s, 2 * m:2 * m + 1, lanes] for s in range(RING)]
                totals = [stats[r, s, 2 * m + 1:2 * m + 2, lanes] for s in range(RING)]
                top = functools.reduce(jnp.maximum, tops)
                total = sum(a * jnp.exp2((b - top) * factor) for a, b in zip(totals, tops))
                own_top = stats[r, x, 2 * m:2 * m + 1, lanes]
                shares.append(jnp.exp2((own_top - top) * factor) / total)
            piece = sums[r, plane, 0] * shares[0] - sums[r, plane, 1] * (shares[1] * lam)
            if d == 0:
                own_piece[r] = piece
            else:
                pieces[r, d] = piece.astype(jnp.bfloat16)
                o1(r, d, d).start()

    def finish(r):
        for d in range(1, RING):
            o1(r, d, d).wait_recv()
        attended = own_piece[r]
        for d in range(1, RING):
            attended = attended + landed[r, d].astype(jnp.float32)
        mean_sq = jnp.mean(attended * attended, axis=0, keepdims=True)
        turned = (attended * lax.rsqrt(mean_sq + EPSILON)).T
        turned = turned * gain_ref[pl.ds(j, 1), :] * (1.0 - LAMBDA_INIT)
        turned_back[r] = turned.astype(jnp.bfloat16).reshape(PLANE, part_rows, value_width)
        for d in range(1, PLANE):
            n1(r, d, j).start()
        normed[j, r] = turned_back[r, j]

    def project(r):
        for d in range(1, PLANE):
            n1(r, d, partner(d)).wait_recv()
        rows = jnp.concatenate([normed[h, r] for h in range(PLANE)], axis=1)

        def product(first):
            return jnp.dot(rows, w_all[:, pl.ds(pl.multiple_of(first, stripe), stripe)], preferred_element_type=jnp.float32)

        def b_stripe(i, carry):
            at = pl.ds(pl.multiple_of(i * stripe, stripe), stripe)
            got = product(area + i * stripe).astype(jnp.bfloat16)
            for side_to in range(SIDES):
                b_out[r, side_to, :, at] = got[side_to * COLUMN * share:(side_to + 1) * COLUMN * share]
            return carry

        def a_stripe(i, carry):
            at = pl.ds(pl.multiple_of(i * stripe, stripe), stripe)
            got = product(i * stripe)
            for y_to in range(COLUMN):
                a_out[r, y_to, :, at] = jnp.concatenate(
                    [got[(s * COLUMN + y_to) * share:(s * COLUMN + y_to + 1) * share] for s in range(SIDES)], axis=0
                ).astype(jnp.bfloat16)
            return carry

        lax.fori_loop(0, area // stripe, b_stripe, 0)
        b1(r).start()
        lax.fori_loop(0, area // stripe, a_stripe, 0)
        for d in (1, 3, 2):
            a1(r, d).start()

    def add_first(r):
        b1(r).wait_recv()

        def b_stripe(i, carry):
            halves = []
            for k in range(2):
                at = pl.ds(pl.multiple_of(k * fold + i * stripe, stripe), stripe)
                halves.append(b_out[r, side, :, at].astype(jnp.float32) + b_in[r, :, at].astype(jnp.float32))
            at = pl.ds(pl.multiple_of(i * stripe, stripe), stripe)
            for y_to in range(COLUMN):
                b2_out[r, y_to, :, at] = jnp.concatenate(
                    [got[y_to * share:(y_to + 1) * share] for got in halves], axis=0).astype(jnp.bfloat16)
            return carry

        lax.fori_loop(0, fold // stripe, b_stripe, 0)
        for d in (1, 3, 2):
            b2(r, d).start()
        for d in range(1, COLUMN):
            a1(r, d).wait_recv()

        def a_stripe(i, carry):
            others = []
            for k in range(2):
                at = pl.ds(pl.multiple_of(k * fold + i * stripe, stripe), stripe)
                got = a_out[r, y, :, at].astype(jnp.float32)
                for d in range(1, COLUMN):
                    got = got + a_in[r, d, :, at].astype(jnp.float32)
                a_mine[r, :, at] = jnp.where(side == 0, got[:share], got[share:])
                others.append(jnp.where(side == 0, got[share:], got[:share]))
            at = pl.ds(pl.multiple_of(i * stripe, stripe), stripe)
            a2_out[r, :, at] = jnp.concatenate(others, axis=0).astype(jnp.bfloat16)
            return carry

        lax.fori_loop(0, fold // stripe, a_stripe, 0)
        a2(r).start()

    def add_last(r):
        for d in range(1, COLUMN):
            b2(r, d).wait_recv()
        a2(r).wait_recv()

        def last_stripe(i, carry):
            at = pl.ds(pl.multiple_of(i * stripe, stripe), stripe)
            a_got = a2_in[r, :, at].astype(jnp.float32)
            b_got = b2_out[r, y, :, at].astype(jnp.float32)
            for d in range(1, COLUMN):
                b_got = b_got + b2_in[r, d, :, at].astype(jnp.float32)
            for k in range(2):
                rows = slice(k * share, (k + 1) * share)
                here = pl.ds(pl.multiple_of(k * fold + i * stripe, stripe), stripe)
                result[r, :, here] = a_mine[r, :, here] + a_got[rows]
                there = pl.ds(pl.multiple_of(area + k * fold + i * stripe, stripe), stripe)
                result[r, :, there] = b_got[rows]
            return carry

        lax.fori_loop(0, fold // stripe, last_stripe, 0)

    stages = ((send_stats, 19), (combine, 23), (finish, 32), (project, 34), (add_first, 45), (add_last, 53))

    def run_stages(n):
        for stage, lag in reversed(stages):
            @pl.when((n >= lag) & (n < lag + PARTS * RING) & (lax.rem(n + 16 * RING - lag, RING) == 0))
            def _():
                stage((n - lag) // RING)

    def start_top(n, m):
        _, r, plane = place(n)
        return stats[r, x, 2 * m:2 * m + 1, pl.ds(pl.multiple_of(plane * tile, tile), tile)]

    top = start_top(0, 0)
    for t in range(steps):
        top = score_step(0, 0, t, 0, top)

    def body(n, top):
        _, r, plane = place(n)
        later = jnp.minimum(n + 1, n_tiles - 1)
        later_d = lax.rem(later, RING)

        @pl.when((n + 1 < half_tiles) & (later_d > 0))
        def _():
            q2(later // RING, later_d, ring_source(later_d)).wait_recv()

        @pl.when(n + 1 == half_tiles)
        def _():
            for d in (2, 3):
                k1(d, partner(d)).wait_recv()
                v1(d, partner(d)).wait_recv()
                v_turned[partner(d)] = v_all[partner(d)].T
            weights_copy.wait()

        lanes = pl.ds(pl.multiple_of(plane * tile, tile), tile)
        for m in range(2):
            following = n if m == 0 else later
            next_top = start_top(following, 1 - m)
            total = jnp.zeros((1, tile), jnp.float32)
            summed = None
            shift = top * factor
            for t in range(steps):
                next_top = score_step(following, 1 - m, t, 1 - m, next_top)
                total, summed = weight_step(n, t, m, shift, total, summed)
            kept = jnp.exp2((stats[r, x, 2 * m:2 * m + 1, lanes] - top) * factor)
            sums[r, plane, m] = sums[r, plane, m] * kept + summed
            stats[r, x, 2 * m:2 * m + 1, lanes] = top
            stats[r, x, 2 * m + 1:2 * m + 2, lanes] = stats[r, x, 2 * m + 1:2 * m + 2, lanes] * kept + total
            top = next_top

        run_stages(n)
        return top

    lax.fori_loop(0, n_tiles, body, top)

    def tail(n, carry):
        run_stages(n)
        return carry

    lax.fori_loop(n_tiles, stages[-1][1] + PARTS * RING, tail, 0)

    def last_waits(r, carry):
        for d in range(1, PLANE):
            n1(r, d, j).wait_send()
        for d in range(1, RING):
            q2(r, d, x).wait_send()
            st(r, d, x).wait_send()
            o1(r, d, d).wait_send()
        for d in range(1, COLUMN):
            a1(r, d).wait_send()
            b2(r, d).wait_send()
        a2(r).wait_send()
        b1(r).wait_send()
        return carry

    lax.fori_loop(0, PARTS, last_waits, 0)
    for d in range(1, PLANE):
        q1(d, j).wait_send()
        k1(d, j).wait_send()
        v1(d, j).wait_send()
    for i in range(columns // stripe):
        at = slice(i * stripe, (i + 1) * stripe)
        out_ref[:, at] = jnp.concatenate([result[r, :, at] for r in range(PARTS)], axis=0).astype(jnp.bfloat16)


def layer(queries, keys, values, spans, lambdas, gain, weights):
    heads, parts, part_rows, width = queries.shape
    held, value_width = values.shape[1:]
    tile = PLANE * part_rows
    tokens = PLANE * held
    vmem = pl.BlockSpec(memory_space=pltpu.VMEM)
    hbm = pl.BlockSpec(memory_space=pl.ANY)
    bf16, f32 = jnp.bfloat16, jnp.float32
    share = part_rows // (COLUMN * SIDES)
    columns = weights.shape[1]
    area = columns // 2
    dma = pltpu.SemaphoreType.DMA
    return pl.pallas_call(
        attention_kernel,
        out_shape=jax.ShapeDtypeStruct((parts * share, columns), bf16),
        in_specs=[hbm, hbm, hbm, vmem, pl.BlockSpec(memory_space=pltpu.SMEM), vmem, hbm],
        out_specs=vmem,
        scratch_shapes=[
            pltpu.VMEM((PARTS, RING, PLANE, part_rows, width), bf16),
            pltpu.VMEM((PLANE, held, width), bf16),
            pltpu.VMEM((PLANE, held, value_width), bf16),
            pltpu.VMEM((PLANE, value_width, held), bf16),
            pltpu.VMEM((2, tokens // HALVES, tile), f32),
            pltpu.VMEM((PARTS, RING, 2, value_width, tile), f32),
            pltpu.VMEM((PARTS, RING, 8, RING * tile), f32),
            pltpu.VMEM((PARTS, RING, value_width, tile), bf16),
            pltpu.VMEM((PARTS, RING, value_width, tile), bf16),
            pltpu.VMEM((PARTS, value_width, tile), f32),
            pltpu.VMEM((PARTS, PLANE, part_rows, value_width), bf16),
            pltpu.VMEM((PLANE, PARTS, part_rows, value_width), bf16),
            pltpu.VMEM(weights.shape, bf16),
            pltpu.VMEM((PARTS, COLUMN, SIDES * share, area), bf16),
            pltpu.VMEM((PARTS, COLUMN, SIDES * share, area), bf16),
            pltpu.VMEM((PARTS, SIDES, COLUMN * share, area), bf16),
            pltpu.VMEM((PARTS, COLUMN * share, area), bf16),
            pltpu.VMEM((PARTS, share, area), f32),
            pltpu.VMEM((PARTS, 2 * share, area // 2), bf16),
            pltpu.VMEM((PARTS, 2 * share, area // 2), bf16),
            pltpu.VMEM((PARTS, COLUMN, 2 * share, area // 2), bf16),
            pltpu.VMEM((PARTS, COLUMN, 2 * share, area // 2), bf16),
            pltpu.VMEM((PARTS, share, columns), f32),
            dma((PLANE,)), dma((PLANE,)), dma((PLANE,)), dma((PLANE,)), dma((PLANE,)), dma((PLANE,)),
            dma((PARTS * RING,)), dma((PARTS * RING,)), dma((PARTS * RING,)), dma((PARTS * RING,)),
            dma((PARTS * RING,)), dma((PARTS * RING,)), dma((PARTS * PLANE,)), dma((PARTS * PLANE,)),
            dma((4,)),
            dma((PARTS * COLUMN,)), dma((PARTS * COLUMN,)), dma((PARTS,)), dma((PARTS,)),
            dma((PARTS,)), dma((PARTS,)), dma((PARTS * COLUMN,)), dma((PARTS * COLUMN,)),
        ],
        compiler_params=pltpu.CompilerParams(
            collective_id=0, has_side_effects=True, vmem_limit_bytes=60 * 1024 * 1024),
    )(queries, keys, values, spans, lambdas, gain, weights)


def per_device(
    queries, cache_keys, cache_values, positions, doc_spans, lambdas, norm_gain, out_weight
):
    q_rows, heads_here, both_width = queries.shape
    part_rows = q_rows // PARTS
    share = part_rows // (COLUMN * SIDES)
    by_head = lambda a: jnp.transpose(a, (1, 0, 2))
    asked = queries.reshape(COLUMN, SIDES, PARTS, share, heads_here, both_width).transpose(4, 2, 1, 0, 3, 5)
    asked = asked.reshape(heads_here, PARTS, part_rows, both_width)
    spans = jnp.stack([doc_spans[:, 0] * BLK, jnp.minimum(positions + 1, doc_spans[:, 1] * BLK)])
    spans = spans.reshape(2, RING, PLANE, COLUMN, SIDES, PARTS, share).transpose(0, 5, 1, 2, 4, 3, 6).reshape(2, -1)
    return layer(
        asked, by_head(cache_keys), by_head(cache_values), spans, lambdas, norm_gain, out_weight)


def solution(mesh):
    placed = (
        P("ctx", "head", None),
        P("ctx", "head", None),
        P("ctx", "head", None),
        P(),
        P(),
        P("head"),
        P("head", None),
        P("head", None),
    )
    return jax.shard_map(
        per_device, mesh=mesh, in_specs=placed, out_specs=P(("ctx", "head"), None), check_vma=False
    )
```

```python
import functools

import jax
import jax.numpy as jnp
from jax import lax
from jax.experimental import pallas as pl
from jax.experimental.pallas import tpu as pltpu
from jax.sharding import PartitionSpec as P

BLK = 128
NEG_BIG = -1e30
TOP_START = -1e29
LAMBDA_INIT = 0.8
EPSILON = 1e-05
LOG2_E = 1.4426950408889634
MESH = pl.DeviceIdType.MESH
PLANE = 4
RING = 4
COLUMN = 4
SIDES = 2
WEIGHTS_AT = 12
PARTS = 4


def attention_kernel(
    q_ref, k_ref, v_ref, span_ref, lam_ref, gain_ref, w_ref, out_ref,
    q_all, k_all, v_all, v_turned, scores, sums, stats, pieces, landed, own_piece, turned_back, normed,
    w_all, a_out, a_in, b_out, b_in, a_mine, a2_out, a2_in, b2_out, b2_in, result,
    q1_send, q1_recv, k_send, k_recv, v_send, v_recv, q2_send, q2_recv,
    st_send, st_recv, o_send, o_recv, n_send, n_recv, local_sem,
    a_send, a_recv, b_send, b_recv, a2_send, a2_recv, b2_send, b2_recv,
):
    ctx = lax.axis_index("ctx")
    head = lax.axis_index("head")
    x = ctx // PLANE
    j = lax.rem(ctx, PLANE)
    y = head // SIDES
    side = lax.rem(head, SIDES)
    part_rows = q_all.shape[3]
    tile = PLANE * part_rows
    held = k_all.shape[1]
    tokens = PLANE * held
    value_width = v_all.shape[2]
    half = q_all.shape[4] // 2
    step = min(256, held)
    steps = tokens // step
    factor = (half ** -0.5) * LOG2_E
    n_tiles = PARTS * RING
    zp = j // 2
    core = lax.rem(j, 2)
    share = part_rows // (COLUMN * SIDES)
    columns = w_ref.shape[1]
    area = columns // 2
    fold = area // 2
    stripe = min(512, fold)

    def partner(k):
        return (2 * zp + 1 - core, 2 * (1 - zp) + core, PLANE - 1 - j)[k - 1]

    def plane_device(k):
        return (x * PLANE + partner(k), head)

    def ring_device(d):
        return (lax.rem(x + d, RING) * PLANE + j, head)

    def column_device(d):
        return (ctx, lax.rem(y + d, COLUMN) * SIDES + side)

    other_side = (ctx, y * SIDES + 1 - side)

    barrier = pltpu.get_barrier_semaphore()
    for d in range(1, PLANE):
        pl.semaphore_signal(barrier, inc=1, device_id=plane_device(d), device_id_type=MESH)
    for d in range(1, RING):
        pl.semaphore_signal(barrier, inc=1, device_id=ring_device(d), device_id_type=MESH)
    for d in range(1, COLUMN):
        pl.semaphore_signal(barrier, inc=1, device_id=column_device(d), device_id_type=MESH)
    pl.semaphore_signal(barrier, inc=1, device_id=other_side, device_id_type=MESH)
    pl.semaphore_wait(barrier, PLANE + RING + COLUMN - 2)

    def q1(r, d, dst):
        return pltpu.make_async_remote_copy(
            q_ref.at[partner(d), r], q_all.at[r, x, dst], q1_send.at[r * PLANE + d], q1_recv.at[r * PLANE + d],
            device_id=plane_device(d), device_id_type=MESH)

    def k1(d, dst):
        return pltpu.make_async_remote_copy(
            k_ref.at[partner(d)], k_all.at[dst], k_send.at[d], k_recv.at[d],
            device_id=plane_device(d), device_id_type=MESH)

    def v1(d, dst):
        return pltpu.make_async_remote_copy(
            v_ref.at[partner(d)], v_all.at[dst], v_send.at[d], v_recv.at[d],
            device_id=plane_device(d), device_id_type=MESH)

    def q2(r, d, dst, far):
        pair = pl.ds(2 * (1 - zp if far else zp), 2)
        at = (r * RING + d) * 2 + far
        return pltpu.make_async_remote_copy(
            q_all.at[r, x, pair], q_all.at[r, dst, pair], q2_send.at[at], q2_recv.at[at],
            device_id=ring_device(RING - d), device_id_type=MESH)

    def st(r, d, dst):
        return pltpu.make_async_remote_copy(
            stats.at[r, x], stats.at[r, dst], st_send.at[r * RING + d], st_recv.at[r * RING + d],
            device_id=ring_device(RING - d), device_id_type=MESH)

    def o1(r, d, dst):
        return pltpu.make_async_remote_copy(
            pieces.at[r, d], landed.at[r, dst], o_send.at[r * RING + d], o_recv.at[r * RING + d],
            device_id=ring_device(RING - d), device_id_type=MESH)

    def n1(r, d, dst):
        return pltpu.make_async_remote_copy(
            turned_back.at[r, partner(d)], normed.at[dst, r], n_send.at[r * PLANE + d], n_recv.at[r * PLANE + d],
            device_id=plane_device(d), device_id_type=MESH)

    def a1(r, d):
        return pltpu.make_async_remote_copy(
            a_out.at[r, lax.rem(y + d, COLUMN)], a_in.at[r, d], a_send.at[r * COLUMN + d], a_recv.at[r * COLUMN + d],
            device_id=column_device(d), device_id_type=MESH)

    def a2(r):
        return pltpu.make_async_remote_copy(
            a2_out.at[r], a2_in.at[r], a2_send.at[r], a2_recv.at[r], device_id=other_side, device_id_type=MESH)

    def b1(r):
        return pltpu.make_async_remote_copy(
            b_out.at[r, 1 - side], b_in.at[r], b_send.at[r], b_recv.at[r], device_id=other_side, device_id_type=MESH)

    def b2(r, d):
        return pltpu.make_async_remote_copy(
            b2_out.at[r, lax.rem(y + d, COLUMN)], b2_in.at[r, d], b2_send.at[r * COLUMN + d], b2_recv.at[r * COLUMN + d],
            device_id=column_device(d), device_id_type=MESH)

    def ring_source(d):
        return lax.rem(x + d, RING)

    def pass_on(r, far):
        for d in (1, 3, 2):
            q2(r, d, x, far).start()

    own_copies = [
        pltpu.make_async_copy(q_ref.at[j], q_all.at[:, x, j], local_sem.at[0]),
        pltpu.make_async_copy(k_ref.at[j], k_all.at[j], local_sem.at[1]),
        pltpu.make_async_copy(v_ref.at[j], v_all.at[j], local_sem.at[2]),
    ]
    own_copies[0].start()
    for d in (2, 3):
        q1(0, d, j).start()
    for r in range(PARTS):
        q1(r, 1, j).start()
    for d in (2, 3):
        k1(d, j).start()
        v1(d, j).start()
    k1(1, j).start()
    v1(1, j).start()
    own_copies[1].start()
    own_copies[2].start()
    weights_copy = pltpu.make_async_copy(w_ref, w_all, local_sem.at[3])
    weights_copy.start()
    own_copies[0].wait()
    q1(0, 1, partner(1)).wait_recv()
    pass_on(0, 0)
    for d in (2, 3):
        q1(0, d, partner(d)).wait_recv()
    pass_on(0, 1)
    for r in range(1, PARTS):
        q1(r, 1, partner(1)).wait_recv()
        pass_on(r, 0)
    own_copies[1].wait()
    own_copies[2].wait()
    k1(1, partner(1)).wait_recv()
    v1(1, partner(1)).wait_recv()
    v_turned[j] = v_all[j].T
    v_turned[partner(1)] = v_all[partner(1)].T
    for d in (2, 3):
        k1(d, partner(d)).wait_recv()
        v1(d, partner(d)).wait_recv()
    for r in range(1, PARTS):
        for d in (2, 3):
            q1(r, d, j).start()
    for d in (2, 3):
        v_turned[partner(d)] = v_all[partner(d)].T

    def far_questions(r):
        for d in (2, 3):
            q1(r + 1, d, partner(d)).wait_recv()
        pass_on(r + 1, 1)

    def place(n):
        return n // RING, lax.rem(x + lax.rem(n, RING), RING)

    def score_step(n, m, t, top):
        r, plane = place(n)
        query = q_all[r, plane, :, :, m * half:(m + 1) * half].reshape(tile, half)
        lanes = pl.ds(pl.multiple_of((r * RING + plane) * tile, tile), tile)
        low = span_ref[0:1, lanes] - x * tokens
        high = span_ref[1:2, lanes] - x * tokens
        first = t * step
        key = k_all[first // held, first % held:first % held + step, m * half:(m + 1) * half]
        s = lax.dot_general(key, query, (((1,), (1,)), ((), ())), preferred_element_type=jnp.float32)
        at = lax.broadcasted_iota(jnp.int32, (step, tile), 0) + first
        s = jnp.where((at >= low) & (at < high), s, NEG_BIG)
        scores[m, first:first + step, :] = s
        return jnp.maximum(top, jnp.max(s, axis=0, keepdims=True))

    def weight_step(m, t, shift, total, summed):
        first = t * step
        w = jnp.exp2(scores[m, first:first + step, :] * factor - shift)
        total = total + jnp.sum(w, axis=0, keepdims=True)
        part = jnp.dot(
            v_turned[first // held, :, first % held:first % held + step], w.astype(jnp.bfloat16),
            preferred_element_type=jnp.float32)
        return total, (part if summed is None else summed + part)

    def send_stats(r):
        for d in range(1, RING):
            st(r, d, x).start()

    def combine(r):
        for d in range(1, RING):
            st(r, d, ring_source(d)).wait_recv()
        lam = lam_ref[j]
        kept = lax.rem(r, 2)
        for d in (1, 3, 2, 0):
            plane = lax.rem(x + RING - d, RING)
            lanes = pl.ds(pl.multiple_of(plane * tile, tile), tile)
            shares = []
            for m in range(2):
                tops = [stats[r, s, 2 * m:2 * m + 1, lanes] for s in range(RING)]
                totals = [stats[r, s, 2 * m + 1:2 * m + 2, lanes] for s in range(RING)]
                top = functools.reduce(jnp.maximum, tops)
                total = sum(a * jnp.exp2((b - top) * factor) for a, b in zip(totals, tops))
                own_top = stats[r, x, 2 * m:2 * m + 1, lanes]
                shares.append(jnp.exp2((own_top - top) * factor) / total)
            piece = sums[kept, plane, 0] * shares[0] - sums[kept, plane, 1] * (shares[1] * lam)
            if d == 0:
                own_piece[r] = piece
            else:
                pieces[r, d] = piece.astype(jnp.bfloat16)
                o1(r, d, d).start()

    def finish(r):
        for d in range(1, RING):
            o1(r, d, d).wait_recv()
        attended = own_piece[r]
        for d in range(1, RING):
            attended = attended + landed[r, d].astype(jnp.float32)
        mean_sq = jnp.mean(attended * attended, axis=0, keepdims=True)
        turned = (attended * lax.rsqrt(mean_sq + EPSILON)).T
        turned = turned * gain_ref[pl.ds(j, 1), :] * (1.0 - LAMBDA_INIT)
        turned_back[r] = turned.astype(jnp.bfloat16).reshape(PLANE, part_rows, value_width)
        for d in range(1, PLANE):
            n1(r, d, j).start()
        normed[j, r] = turned_back[r, j]

    def project(r):
        for d in range(1, PLANE):
            n1(r, d, partner(d)).wait_recv()
        rows = jnp.concatenate([normed[h, r] for h in range(PLANE)], axis=1)

        def product(first):
            return jnp.dot(rows, w_all[:, pl.ds(pl.multiple_of(first, stripe), stripe)], preferred_element_type=jnp.float32)

        def b_stripe(i, carry):
            at = pl.ds(pl.multiple_of(i * stripe, stripe), stripe)
            got = product(area + i * stripe).astype(jnp.bfloat16)
            for side_to in range(SIDES):
                b_out[r, side_to, :, at] = got[side_to * COLUMN * share:(side_to + 1) * COLUMN * share]
            return carry

        def a_stripe(i, carry):
            at = pl.ds(pl.multiple_of(i * stripe, stripe), stripe)
            got = product(i * stripe)
            for y_to in range(COLUMN):
                a_out[r, y_to, :, at] = jnp.concatenate(
                    [got[(s * COLUMN + y_to) * share:(s * COLUMN + y_to + 1) * share] for s in range(SIDES)], axis=0
                ).astype(jnp.bfloat16)
            return carry

        lax.fori_loop(0, area // stripe, b_stripe, 0)
        b1(r).start()
        lax.fori_loop(0, area // stripe, a_stripe, 0)
        for d in (1, 3, 2):
            a1(r, d).start()

    def add_first(r):
        b1(r).wait_recv()

        def b_stripe(i, carry):
            halves = []
            for k in range(2):
                at = pl.ds(pl.multiple_of(k * fold + i * stripe, stripe), stripe)
                halves.append(b_out[r, side, :, at].astype(jnp.float32) + b_in[r, :, at].astype(jnp.float32))
            at = pl.ds(pl.multiple_of(i * stripe, stripe), stripe)
            for y_to in range(COLUMN):
                b2_out[r, y_to, :, at] = jnp.concatenate(
                    [got[y_to * share:(y_to + 1) * share] for got in halves], axis=0).astype(jnp.bfloat16)
            return carry

        lax.fori_loop(0, fold // stripe, b_stripe, 0)
        for d in (1, 3, 2):
            b2(r, d).start()
        for d in range(1, COLUMN):
            a1(r, d).wait_recv()

        def a_stripe(i, carry):
            others = []
            for k in range(2):
                at = pl.ds(pl.multiple_of(k * fold + i * stripe, stripe), stripe)
                got = a_out[r, y, :, at].astype(jnp.float32)
                for d in range(1, COLUMN):
                    got = got + a_in[r, d, :, at].astype(jnp.float32)
                a_mine[r, :, at] = jnp.where(side == 0, got[:share], got[share:])
                others.append(jnp.where(side == 0, got[share:], got[:share]))
            at = pl.ds(pl.multiple_of(i * stripe, stripe), stripe)
            a2_out[r, :, at] = jnp.concatenate(others, axis=0).astype(jnp.bfloat16)
            return carry

        lax.fori_loop(0, fold // stripe, a_stripe, 0)
        a2(r).start()

    def add_last(r):
        for d in range(1, COLUMN):
            b2(r, d).wait_recv()
        a2(r).wait_recv()

        def last_stripe(i, carry):
            at = pl.ds(pl.multiple_of(i * stripe, stripe), stripe)
            a_got = a2_in[r, :, at].astype(jnp.float32)
            b_got = b2_out[r, y, :, at].astype(jnp.float32)
            for d in range(1, COLUMN):
                b_got = b_got + b2_in[r, d, :, at].astype(jnp.float32)
            for k in range(2):
                rows = slice(k * share, (k + 1) * share)
                here = pl.ds(pl.multiple_of(k * fold + i * stripe, stripe), stripe)
                result[r, :, here] = a_mine[r, :, here] + a_got[rows]
                there = pl.ds(pl.multiple_of(area + k * fold + i * stripe, stripe), stripe)
                result[r, :, there] = b_got[rows]
            return carry

        lax.fori_loop(0, fold // stripe, last_stripe, 0)

    stages = ((send_stats, 3), (combine, 5), (finish, 11), (project, 14), (add_first, 20), (add_last, 24))

    def run_stages(n):
        for stage, lag in reversed(stages):
            @pl.when((n >= lag) & (n < lag + n_tiles) & (lax.rem(n + 16 * RING - lag, RING) == 0))
            def _():
                stage((n - lag) // RING)

    first_top = jnp.full((1, tile), TOP_START, jnp.float32)
    top = first_top
    for t in range(steps):
        top = score_step(0, 0, t, top)

    def body(n, top):
        r, plane = place(n)
        later = jnp.minimum(n + 1, n_tiles - 1)
        later_r, later_d = later // RING, lax.rem(later, RING)

        @pl.when((lax.rem(n, RING) == 1) & (r + 1 < PARTS))
        def _():
            far_questions(r)

        @pl.when((n + 1 < n_tiles) & (later_d > 0))
        def _():
            for far in range(2):
                q2(later_r, later_d, ring_source(later_d), far).wait_recv()

        lanes = pl.ds(pl.multiple_of(plane * tile, tile), tile)
        for m in range(2):
            next_top = first_top
            total = jnp.zeros((1, tile), jnp.float32)
            summed = None
            shift = top * factor
            for t in range(steps):
                next_top = score_step(n if m == 0 else later, 1 - m, t, next_top)
                total, summed = weight_step(m, t, shift, total, summed)
            sums[lax.rem(r, 2), plane, m] = summed
            stats[r, x, 2 * m:2 * m + 1, lanes] = top
            stats[r, x, 2 * m + 1:2 * m + 2, lanes] = total
            top = next_top

        @pl.when(n == WEIGHTS_AT)
        def _():
            weights_copy.wait()

        run_stages(n)
        return top

    lax.fori_loop(0, n_tiles, body, top)

    def tail(n, carry):
        run_stages(n)
        return carry

    lax.fori_loop(n_tiles, stages[-1][1] + n_tiles - RING + 1, tail, 0)

    def last_waits(r, carry):
        for d in range(1, PLANE):
            n1(r, d, j).wait_send()
            q1(r, d, j).wait_send()
        for d in range(1, RING):
            q2(r, d, x, 0).wait_send()
            q2(r, d, x, 1).wait_send()
            st(r, d, x).wait_send()
            o1(r, d, d).wait_send()
        for d in range(1, COLUMN):
            a1(r, d).wait_send()
            b2(r, d).wait_send()
        a2(r).wait_send()
        b1(r).wait_send()
        return carry

    lax.fori_loop(0, PARTS, last_waits, 0)
    for d in range(1, PLANE):
        k1(d, j).wait_send()
        v1(d, j).wait_send()
    for i in range(columns // stripe):
        at = slice(i * stripe, (i + 1) * stripe)
        out_ref[:, at] = jnp.concatenate([result[r, :, at] for r in range(PARTS)], axis=0).astype(jnp.bfloat16)


def layer(queries, keys, values, spans, lambdas, gain, weights):
    heads, parts, part_rows, width = queries.shape
    held, value_width = values.shape[1:]
    tile = PLANE * part_rows
    tokens = PLANE * held
    vmem = pl.BlockSpec(memory_space=pltpu.VMEM)
    hbm = pl.BlockSpec(memory_space=pl.ANY)
    bf16, f32 = jnp.bfloat16, jnp.float32
    share = part_rows // (COLUMN * SIDES)
    columns = weights.shape[1]
    area = columns // 2
    dma = pltpu.SemaphoreType.DMA
    return pl.pallas_call(
        attention_kernel,
        out_shape=jax.ShapeDtypeStruct((parts * share, columns), bf16),
        in_specs=[hbm, hbm, hbm, vmem, pl.BlockSpec(memory_space=pltpu.SMEM), vmem, hbm],
        out_specs=vmem,
        scratch_shapes=[
            pltpu.VMEM((PARTS, RING, PLANE, part_rows, width), bf16),
            pltpu.VMEM((PLANE, held, width), bf16),
            pltpu.VMEM((PLANE, held, value_width), bf16),
            pltpu.VMEM((PLANE, value_width, held), bf16),
            pltpu.VMEM((2, tokens, tile), f32),
            pltpu.VMEM((2, RING, 2, value_width, tile), f32),
            pltpu.VMEM((PARTS, RING, 8, RING * tile), f32),
            pltpu.VMEM((PARTS, RING, value_width, tile), bf16),
            pltpu.VMEM((PARTS, RING, value_width, tile), bf16),
            pltpu.VMEM((PARTS, value_width, tile), f32),
            pltpu.VMEM((PARTS, PLANE, part_rows, value_width), bf16),
            pltpu.VMEM((PLANE, PARTS, part_rows, value_width), bf16),
            pltpu.VMEM(weights.shape, bf16),
            pltpu.VMEM((PARTS, COLUMN, SIDES * share, area), bf16),
            pltpu.VMEM((PARTS, COLUMN, SIDES * share, area), bf16),
            pltpu.VMEM((PARTS, SIDES, COLUMN * share, area), bf16),
            pltpu.VMEM((PARTS, COLUMN * share, area), bf16),
            pltpu.VMEM((PARTS, share, area), f32),
            pltpu.VMEM((PARTS, 2 * share, area // 2), bf16),
            pltpu.VMEM((PARTS, 2 * share, area // 2), bf16),
            pltpu.VMEM((PARTS, COLUMN, 2 * share, area // 2), bf16),
            pltpu.VMEM((PARTS, COLUMN, 2 * share, area // 2), bf16),
            pltpu.VMEM((PARTS, share, columns), f32),
            dma((PARTS * PLANE,)), dma((PARTS * PLANE,)), dma((PLANE,)), dma((PLANE,)), dma((PLANE,)), dma((PLANE,)),
            dma((2 * PARTS * RING,)), dma((2 * PARTS * RING,)), dma((PARTS * RING,)), dma((PARTS * RING,)),
            dma((PARTS * RING,)), dma((PARTS * RING,)), dma((PARTS * PLANE,)), dma((PARTS * PLANE,)),
            dma((4,)),
            dma((PARTS * COLUMN,)), dma((PARTS * COLUMN,)), dma((PARTS,)), dma((PARTS,)),
            dma((PARTS,)), dma((PARTS,)), dma((PARTS * COLUMN,)), dma((PARTS * COLUMN,)),
        ],
        compiler_params=pltpu.CompilerParams(
            collective_id=0, has_side_effects=True, vmem_limit_bytes=60 * 1024 * 1024),
    )(queries, keys, values, spans, lambdas, gain, weights)


def per_device(
    queries, cache_keys, cache_values, positions, doc_spans, lambdas, norm_gain, out_weight
):
    q_rows, heads_here, both_width = queries.shape
    part_rows = q_rows // PARTS
    share = part_rows // (COLUMN * SIDES)
    by_head = lambda a: jnp.transpose(a, (1, 0, 2))
    asked = queries.reshape(COLUMN, SIDES, PARTS, share, heads_here, both_width).transpose(4, 2, 1, 0, 3, 5)
    asked = asked.reshape(heads_here, PARTS, part_rows, both_width)
    spans = jnp.stack([doc_spans[:, 0] * BLK, jnp.minimum(positions + 1, doc_spans[:, 1] * BLK)])
    spans = spans.reshape(2, RING, PLANE, COLUMN, SIDES, PARTS, share).transpose(0, 5, 1, 2, 4, 3, 6).reshape(2, -1)
    return layer(
        asked, by_head(cache_keys), by_head(cache_values), spans, lambdas, norm_gain, out_weight)


def solution(mesh):
    placed = (
        P("ctx", "head", None),
        P("ctx", "head", None),
        P("ctx", "head", None),
        P(),
        P(),
        P("head"),
        P("head", None),
        P("head", None),
    )
    return jax.shard_map(
        per_device, mesh=mesh, in_specs=placed, out_specs=P(("ctx", "head"), None), check_vma=False
    )
```

```python
import functools

import jax
import jax.numpy as jnp
from jax import lax
from jax.experimental import pallas as pl
from jax.experimental.pallas import tpu as pltpu
from jax.sharding import PartitionSpec as P

BLK = 128
NEG_BIG = -1e30
TOP_START = -1e29
LAMBDA_INIT = 0.8
EPSILON = 1e-05
LOG2_E = 1.4426950408889634
MESH = pl.DeviceIdType.MESH
PLANE = 4
RING = 4
COLUMN = 4
SIDES = 2
HALVES = 2
PARTS = 4


def attention_kernel(
    q_ref, k_ref, v_ref, span_ref, lam_ref, gain_ref, w_ref, out_ref,
    q_all, k_all, v_all, v_turned, scores, sums, stats, pieces, landed, own_piece, turned_back, normed,
    w_all, a_out, a_in, b_out, b_in, a_mine, a2_out, a2_in, b2_out, b2_in, result,
    q1_send, q1_recv, k_send, k_recv, v_send, v_recv, q2_send, q2_recv,
    st_send, st_recv, o_send, o_recv, n_send, n_recv, local_sem,
    a_send, a_recv, b_send, b_recv, a2_send, a2_recv, b2_send, b2_recv,
):
    ctx = lax.axis_index("ctx")
    head = lax.axis_index("head")
    x = ctx // PLANE
    j = lax.rem(ctx, PLANE)
    y = head // SIDES
    side = lax.rem(head, SIDES)
    part_rows = q_all.shape[3]
    tile = PLANE * part_rows
    held = k_all.shape[1]
    tokens = PLANE * held
    near = tokens // HALVES
    value_width = v_all.shape[2]
    half = q_all.shape[4] // 2
    step = min(256, held)
    steps = near // step
    factor = (half ** -0.5) * LOG2_E
    half_tiles = PARTS * RING
    n_tiles = HALVES * half_tiles
    zp = j // 2
    core = lax.rem(j, 2)
    share = part_rows // (COLUMN * SIDES)
    columns = w_ref.shape[1]
    area = columns // 2
    fold = area // 2
    stripe = min(512, fold)
    wide = min(2048, area)

    def partner(k):
        return (2 * zp + 1 - core, 2 * (1 - zp) + core, PLANE - 1 - j)[k - 1]

    def plane_device(k):
        return (x * PLANE + partner(k), head)

    def ring_device(d):
        return (lax.rem(x + d, RING) * PLANE + j, head)

    def column_device(d):
        return (ctx, lax.rem(y + d, COLUMN) * SIDES + side)

    other_side = (ctx, y * SIDES + 1 - side)

    barrier = pltpu.get_barrier_semaphore()
    for d in range(1, PLANE):
        pl.semaphore_signal(barrier, inc=1, device_id=plane_device(d), device_id_type=MESH)
    for d in range(1, RING):
        pl.semaphore_signal(barrier, inc=1, device_id=ring_device(d), device_id_type=MESH)
    for d in range(1, COLUMN):
        pl.semaphore_signal(barrier, inc=1, device_id=column_device(d), device_id_type=MESH)
    pl.semaphore_signal(barrier, inc=1, device_id=other_side, device_id_type=MESH)
    pl.semaphore_wait(barrier, PLANE + RING + COLUMN - 2)

    def q1(d, dst):
        return pltpu.make_async_remote_copy(
            q_ref.at[partner(d)], q_all.at[:, x, dst], q1_send.at[d], q1_recv.at[d],
            device_id=plane_device(d), device_id_type=MESH)

    def k1(d, dst):
        return pltpu.make_async_remote_copy(
            k_ref.at[partner(d)], k_all.at[dst], k_send.at[d], k_recv.at[d],
            device_id=plane_device(d), device_id_type=MESH)

    def v1(d, dst):
        return pltpu.make_async_remote_copy(
            v_ref.at[partner(d)], v_all.at[dst], v_send.at[d], v_recv.at[d],
            device_id=plane_device(d), device_id_type=MESH)

    def q2(r, d, dst, far):
        pair = pl.ds(2 * (1 - zp if far else zp), 2)
        at = (r * RING + d) * 2 + far
        return pltpu.make_async_remote_copy(
            q_all.at[r, x, pair], q_all.at[r, dst, pair], q2_send.at[at], q2_recv.at[at],
            device_id=ring_device(RING - d), device_id_type=MESH)

    def st(r, d, dst):
        return pltpu.make_async_remote_copy(
            stats.at[r, x], stats.at[r, dst], st_send.at[r * RING + d], st_recv.at[r * RING + d],
            device_id=ring_device(RING - d), device_id_type=MESH)

    def o1(r, d, dst):
        return pltpu.make_async_remote_copy(
            pieces.at[r, d], landed.at[r, dst], o_send.at[r * RING + d], o_recv.at[r * RING + d],
            device_id=ring_device(RING - d), device_id_type=MESH)

    def n1(r, d, dst):
        return pltpu.make_async_remote_copy(
            turned_back.at[r, partner(d)], normed.at[dst, r], n_send.at[r * PLANE + d], n_recv.at[r * PLANE + d],
            device_id=plane_device(d), device_id_type=MESH)

    def a1(r, d):
        return pltpu.make_async_remote_copy(
            a_out.at[r, lax.rem(y + d, COLUMN)], a_in.at[r, d], a_send.at[r * COLUMN + d], a_recv.at[r * COLUMN + d],
            device_id=column_device(d), device_id_type=MESH)

    def a2(r):
        return pltpu.make_async_remote_copy(
            a2_out.at[r], a2_in.at[r], a2_send.at[r], a2_recv.at[r], device_id=other_side, device_id_type=MESH)

    def b1(r):
        return pltpu.make_async_remote_copy(
            b_out.at[r, 1 - side], b_in.at[r], b_send.at[r], b_recv.at[r], device_id=other_side, device_id_type=MESH)

    def b2(r, d):
        return pltpu.make_async_remote_copy(
            b2_out.at[r, lax.rem(y + d, COLUMN)], b2_in.at[r, d], b2_send.at[r * COLUMN + d], b2_recv.at[r * COLUMN + d],
            device_id=column_device(d), device_id_type=MESH)

    def ring_source(d):
        return lax.rem(x + d, RING)

    def pass_on(r, far):
        for d in (1, 3, 2):
            q2(r, d, x, far).start()

    own_copies = [
        pltpu.make_async_copy(q_ref.at[j], q_all.at[:, x, j], local_sem.at[0]),
        pltpu.make_async_copy(k_ref.at[j], k_all.at[j], local_sem.at[1]),
        pltpu.make_async_copy(v_ref.at[j], v_all.at[j], local_sem.at[2]),
    ]
    own_copies[0].start()
    for d in (1, 2, 3):
        q1(d, j).start()
    for d in (2, 3, 1):
        k1(d, j).start()
        v1(d, j).start()
    own_copies[1].start()
    own_copies[2].start()
    weights_copy = pltpu.make_async_copy(w_ref, w_all, local_sem.at[3])
    weights_copy.start()
    own_copies[0].wait()
    q1(1, partner(1)).wait_recv()
    pass_on(0, 0)
    pass_on(1, 0)

    def clear(i, carry):
        r, plane = i // RING, lax.rem(i, RING)
        sums[r, plane] = jnp.zeros(sums.shape[2:], jnp.float32)
        lanes = pl.ds(pl.multiple_of(plane * tile, tile), tile)
        for m in range(2):
            stats[r, x, 2 * m:2 * m + 1, lanes] = jnp.full((1, tile), TOP_START, jnp.float32)
            stats[r, x, 2 * m + 1:2 * m + 2, lanes] = jnp.zeros((1, tile), jnp.float32)
        return carry

    lax.fori_loop(0, half_tiles, clear, 0)
    for d in (2, 3):
        q1(d, partner(d)).wait_recv()
    pass_on(0, 1)
    pass_on(1, 1)
    for r in range(2, PARTS):
        pass_on(r, 0)
        pass_on(r, 1)
    own_copies[1].wait()
    own_copies[2].wait()
    k1(1, partner(1)).wait_recv()
    v1(1, partner(1)).wait_recv()
    for source in (j, partner(1)):
        v_turned[source] = v_all[source].T

    def place(n):
        late = n // half_tiles
        at = lax.rem(n, half_tiles)
        return 2 * (zp + late - 2 * zp * late), at // RING, lax.rem(x + lax.rem(at, RING), RING)

    def score_step(n, m, t, slot, top):
        source, r, plane = place(n)
        query = q_all[r, plane, :, :, m * half:(m + 1) * half].reshape(tile, half)
        lanes = pl.ds(pl.multiple_of((r * RING + plane) * tile, tile), tile)
        base = x * tokens + source * held
        low = span_ref[0:1, lanes] - base
        high = span_ref[1:2, lanes] - base
        first = t * step
        key = k_all[source + first // held, first % held:first % held + step, m * half:(m + 1) * half]
        s = lax.dot_general(key, query, (((1,), (1,)), ((), ())), preferred_element_type=jnp.float32)
        at = lax.broadcasted_iota(jnp.int32, (step, tile), 0) + first
        s = jnp.where((at >= low) & (at < high), s, NEG_BIG)
        scores[slot, first:first + step, :] = s
        return jnp.maximum(top, jnp.max(s, axis=0, keepdims=True))

    def weight_step(n, t, slot, shift, total, summed):
        source, _, _ = place(n)
        first = t * step
        w = jnp.exp2(scores[slot, first:first + step, :] * factor - shift)
        total = total + jnp.sum(w, axis=0, keepdims=True)
        part = jnp.dot(
            v_turned[source + first // held, :, first % held:first % held + step], w.astype(jnp.bfloat16),
            preferred_element_type=jnp.float32)
        return total, (part if summed is None else summed + part)

    def send_stats(r):
        for d in range(1, RING):
            st(r, d, x).start()

    def combine(r):
        for d in range(1, RING):
            st(r, d, ring_source(d)).wait_recv()
        lam = lam_ref[j]
        for d in (1, 3, 2, 0):
            plane = lax.rem(x + RING - d, RING)
            lanes = pl.ds(pl.multiple_of(plane * tile, tile), tile)
            shares = []
            for m in range(2):
                tops = [stats[r, s, 2 * m:2 * m + 1, lanes] for s in range(RING)]
                totals = [stats[r, s, 2 * m + 1:2 * m + 2, lanes] for s in range(RING)]
                top = functools.reduce(jnp.maximum, tops)
                total = sum(a * jnp.exp2((b - top) * factor) for a, b in zip(totals, tops))
                own_top = stats[r, x, 2 * m:2 * m + 1, lanes]
                shares.append(jnp.exp2((own_top - top) * factor) / total)
            piece = sums[r, plane, 0] * shares[0] - sums[r, plane, 1] * (shares[1] * lam)
            if d == 0:
                own_piece[r] = piece
            else:
                pieces[r, d] = piece.astype(jnp.bfloat16)
                o1(r, d, d).start()

    def finish(r):
        for d in range(1, RING):
            o1(r, d, d).wait_recv()
        attended = own_piece[r]
        for d in range(1, RING):
            attended = attended + landed[r, d].astype(jnp.float32)
        mean_sq = jnp.mean(attended * attended, axis=0, keepdims=True)
        turned = (attended * lax.rsqrt(mean_sq + EPSILON)).T
        turned = turned * gain_ref[pl.ds(j, 1), :] * (1.0 - LAMBDA_INIT)
        turned_back[r] = turned.astype(jnp.bfloat16).reshape(PLANE, part_rows, value_width)
        for d in range(1, PLANE):
            n1(r, d, j).start()
        normed[j, r] = turned_back[r, j]

    def project(r):
        for d in range(1, PLANE):
            n1(r, d, partner(d)).wait_recv()
        rows = jnp.concatenate([normed[h, r] for h in range(PLANE)], axis=1)

        def product(first):
            return jnp.dot(rows, w_all[:, pl.ds(pl.multiple_of(first, wide), wide)], preferred_element_type=jnp.float32)

        def b_wide(i, carry):
            at = pl.ds(pl.multiple_of(i * wide, wide), wide)
            got = product(area + i * wide).astype(jnp.bfloat16)
            for side_to in range(SIDES):
                b_out[r, side_to, :, at] = got[side_to * COLUMN * share:(side_to + 1) * COLUMN * share]
            return carry

        def a_wide(i, carry):
            at = pl.ds(pl.multiple_of(i * wide, wide), wide)
            got = product(i * wide)
            for y_to in range(COLUMN):
                a_out[r, y_to, :, at] = jnp.concatenate(
                    [got[(s * COLUMN + y_to) * share:(s * COLUMN + y_to + 1) * share] for s in range(SIDES)], axis=0
                ).astype(jnp.bfloat16)
            return carry

        lax.fori_loop(0, area // wide, b_wide, 0)
        b1(r).start()
        lax.fori_loop(0, area // wide, a_wide, 0)
        for d in (1, 3, 2):
            a1(r, d).start()

    def add_first(r):
        b1(r).wait_recv()

        def b_stripe(i, carry):
            halves = []
            for k in range(2):
                at = pl.ds(pl.multiple_of(k * fold + i * stripe, stripe), stripe)
                halves.append(b_out[r, side, :, at].astype(jnp.float32) + b_in[r, :, at].astype(jnp.float32))
            at = pl.ds(pl.multiple_of(i * stripe, stripe), stripe)
            for y_to in range(COLUMN):
                b2_out[r, y_to, :, at] = jnp.concatenate(
                    [got[y_to * share:(y_to + 1) * share] for got in halves], axis=0).astype(jnp.bfloat16)
            return carry

        lax.fori_loop(0, fold // stripe, b_stripe, 0)
        for d in (1, 3, 2):
            b2(r, d).start()
        for d in range(1, COLUMN):
            a1(r, d).wait_recv()

        def a_stripe(i, carry):
            others = []
            for k in range(2):
                at = pl.ds(pl.multiple_of(k * fold + i * stripe, stripe), stripe)
                got = a_out[r, y, :, at].astype(jnp.float32)
                for d in range(1, COLUMN):
                    got = got + a_in[r, d, :, at].astype(jnp.float32)
                a_mine[r, :, at] = jnp.where(side == 0, got[:share], got[share:])
                others.append(jnp.where(side == 0, got[share:], got[:share]))
            at = pl.ds(pl.multiple_of(i * stripe, stripe), stripe)
            a2_out[r, :, at] = jnp.concatenate(others, axis=0).astype(jnp.bfloat16)
            return carry

        lax.fori_loop(0, fold // stripe, a_stripe, 0)
        a2(r).start()

    def add_last(r):
        for d in range(1, COLUMN):
            b2(r, d).wait_recv()
        a2(r).wait_recv()

        def last_stripe(i, carry):
            at = pl.ds(pl.multiple_of(i * stripe, stripe), stripe)
            a_got = a2_in[r, :, at].astype(jnp.float32)
            b_got = b2_out[r, y, :, at].astype(jnp.float32)
            for d in range(1, COLUMN):
                b_got = b_got + b2_in[r, d, :, at].astype(jnp.float32)
            for k in range(2):
                rows = slice(k * share, (k + 1) * share)
                here = pl.ds(pl.multiple_of(k * fold + i * stripe, stripe), stripe)
                result[r, :, here] = a_mine[r, :, here] + a_got[rows]
                there = pl.ds(pl.multiple_of(area + k * fold + i * stripe, stripe), stripe)
                result[r, :, there] = b_got[rows]
            return carry

        lax.fori_loop(0, fold // stripe, last_stripe, 0)

    stages = ((send_stats, 19), (combine, 24), (finish, 33), (project, 36), (add_first, 41), (add_last, 50))

    def run_stages(n):
        for stage, lag in reversed(stages):
            @pl.when((n >= lag) & (n < lag + PARTS * RING) & (lax.rem(n + 16 * RING - lag, RING) == 0))
            def _():
                stage((n - lag) // RING)

    def start_top(n, m):
        _, r, plane = place(n)
        return stats[r, x, 2 * m:2 * m + 1, pl.ds(pl.multiple_of(plane * tile, tile), tile)]

    top = start_top(0, 0)
    for t in range(steps):
        top = score_step(0, 0, t, 0, top)

    def body(n, top):
        _, r, plane = place(n)
        later = jnp.minimum(n + 1, n_tiles - 1)
        later_d = lax.rem(later, RING)

        @pl.when((n + 1 < half_tiles) & (later_d > 0))
        def _():
            for far in range(2):
                q2(later // RING, later_d, ring_source(later_d), far).wait_recv()

        @pl.when(n + 1 == half_tiles)
        def _():
            for d in (2, 3):
                k1(d, partner(d)).wait_recv()
                v1(d, partner(d)).wait_recv()
                v_turned[partner(d)] = v_all[partner(d)].T
            weights_copy.wait()

        lanes = pl.ds(pl.multiple_of(plane * tile, tile), tile)
        for m in range(2):
            following = n if m == 0 else later
            next_top = start_top(following, 1 - m)
            total = jnp.zeros((1, tile), jnp.float32)
            summed = None
            shift = top * factor
            for t in range(steps):
                next_top = score_step(following, 1 - m, t, 1 - m, next_top)
                total, summed = weight_step(n, t, m, shift, total, summed)
            kept = jnp.exp2((stats[r, x, 2 * m:2 * m + 1, lanes] - top) * factor)
            sums[r, plane, m] = sums[r, plane, m] * kept + summed
            stats[r, x, 2 * m:2 * m + 1, lanes] = top
            stats[r, x, 2 * m + 1:2 * m + 2, lanes] = stats[r, x, 2 * m + 1:2 * m + 2, lanes] * kept + total
            top = next_top

        run_stages(n)
        return top

    lax.fori_loop(0, n_tiles, body, top)

    def tail(n, carry):
        run_stages(n)
        return carry

    lax.fori_loop(n_tiles, stages[-1][1] + PARTS * RING, tail, 0)

    def last_waits(r, carry):
        for d in range(1, PLANE):
            n1(r, d, j).wait_send()
        for d in range(1, RING):
            q2(r, d, x, 0).wait_send()
            q2(r, d, x, 1).wait_send()
            st(r, d, x).wait_send()
            o1(r, d, d).wait_send()
        for d in range(1, COLUMN):
            a1(r, d).wait_send()
            b2(r, d).wait_send()
        a2(r).wait_send()
        b1(r).wait_send()
        return carry

    lax.fori_loop(0, PARTS, last_waits, 0)
    for d in range(1, PLANE):
        q1(d, j).wait_send()
        k1(d, j).wait_send()
        v1(d, j).wait_send()
    for i in range(columns // stripe):
        at = slice(i * stripe, (i + 1) * stripe)
        out_ref[:, at] = jnp.concatenate([result[r, :, at] for r in range(PARTS)], axis=0).astype(jnp.bfloat16)


def layer(queries, keys, values, spans, lambdas, gain, weights):
    heads, parts, part_rows, width = queries.shape
    held, value_width = values.shape[1:]
    tile = PLANE * part_rows
    tokens = PLANE * held
    vmem = pl.BlockSpec(memory_space=pltpu.VMEM)
    hbm = pl.BlockSpec(memory_space=pl.ANY)
    bf16, f32 = jnp.bfloat16, jnp.float32
    share = part_rows // (COLUMN * SIDES)
    columns = weights.shape[1]
    area = columns // 2
    dma = pltpu.SemaphoreType.DMA
    return pl.pallas_call(
        attention_kernel,
        out_shape=jax.ShapeDtypeStruct((parts * share, columns), bf16),
        in_specs=[hbm, hbm, hbm, vmem, pl.BlockSpec(memory_space=pltpu.SMEM), vmem, hbm],
        out_specs=vmem,
        scratch_shapes=[
            pltpu.VMEM((PARTS, RING, PLANE, part_rows, width), bf16),
            pltpu.VMEM((PLANE, held, width), bf16),
            pltpu.VMEM((PLANE, held, value_width), bf16),
            pltpu.VMEM((PLANE, value_width, held), bf16),
            pltpu.VMEM((2, tokens // HALVES, tile), f32),
            pltpu.VMEM((PARTS, RING, 2, value_width, tile), f32),
            pltpu.VMEM((PARTS, RING, 8, RING * tile), f32),
            pltpu.VMEM((PARTS, RING, value_width, tile), bf16),
            pltpu.VMEM((PARTS, RING, value_width, tile), bf16),
            pltpu.VMEM((PARTS, value_width, tile), f32),
            pltpu.VMEM((PARTS, PLANE, part_rows, value_width), bf16),
            pltpu.VMEM((PLANE, PARTS, part_rows, value_width), bf16),
            pltpu.VMEM(weights.shape, bf16),
            pltpu.VMEM((PARTS, COLUMN, SIDES * share, area), bf16),
            pltpu.VMEM((PARTS, COLUMN, SIDES * share, area), bf16),
            pltpu.VMEM((PARTS, SIDES, COLUMN * share, area), bf16),
            pltpu.VMEM((PARTS, COLUMN * share, area), bf16),
            pltpu.VMEM((PARTS, share, area), f32),
            pltpu.VMEM((PARTS, 2 * share, area // 2), bf16),
            pltpu.VMEM((PARTS, 2 * share, area // 2), bf16),
            pltpu.VMEM((PARTS, COLUMN, 2 * share, area // 2), bf16),
            pltpu.VMEM((PARTS, COLUMN, 2 * share, area // 2), bf16),
            pltpu.VMEM((PARTS, share, columns), f32),
            dma((PLANE,)), dma((PLANE,)), dma((PLANE,)), dma((PLANE,)), dma((PLANE,)), dma((PLANE,)),
            dma((2 * PARTS * RING,)), dma((2 * PARTS * RING,)), dma((PARTS * RING,)), dma((PARTS * RING,)),
            dma((PARTS * RING,)), dma((PARTS * RING,)), dma((PARTS * PLANE,)), dma((PARTS * PLANE,)),
            dma((4,)),
            dma((PARTS * COLUMN,)), dma((PARTS * COLUMN,)), dma((PARTS,)), dma((PARTS,)),
            dma((PARTS,)), dma((PARTS,)), dma((PARTS * COLUMN,)), dma((PARTS * COLUMN,)),
        ],
        compiler_params=pltpu.CompilerParams(
            collective_id=0, has_side_effects=True, vmem_limit_bytes=60 * 1024 * 1024),
    )(queries, keys, values, spans, lambdas, gain, weights)


def per_device(
    queries, cache_keys, cache_values, positions, doc_spans, lambdas, norm_gain, out_weight
):
    q_rows, heads_here, both_width = queries.shape
    part_rows = q_rows // PARTS
    share = part_rows // (COLUMN * SIDES)
    by_head = lambda a: jnp.transpose(a, (1, 0, 2))
    asked = queries.reshape(COLUMN, SIDES, PARTS, share, heads_here, both_width).transpose(4, 2, 1, 0, 3, 5)
    asked = asked.reshape(heads_here, PARTS, part_rows, both_width)
    spans = jnp.stack([doc_spans[:, 0] * BLK, jnp.minimum(positions + 1, doc_spans[:, 1] * BLK)])
    spans = spans.reshape(2, RING, PLANE, COLUMN, SIDES, PARTS, share).transpose(0, 5, 1, 2, 4, 3, 6).reshape(2, -1)
    return layer(
        asked, by_head(cache_keys), by_head(cache_values), spans, lambdas, norm_gain, out_weight)


def solution(mesh):
    placed = (
        P("ctx", "head", None),
        P("ctx", "head", None),
        P("ctx", "head", None),
        P(),
        P(),
        P("head"),
        P("head", None),
        P("head", None),
    )
    return jax.shard_map(
        per_device, mesh=mesh, in_specs=placed, out_specs=P(("ctx", "head"), None), check_vma=False
    )
```

```python
import functools

import jax
import jax.numpy as jnp
from jax import lax
from jax.experimental import pallas as pl
from jax.experimental.pallas import tpu as pltpu
from jax.sharding import PartitionSpec as P

BLK = 128
NEG_BIG = -1e30
TOP_START = -1e29
LAMBDA_INIT = 0.8
EPSILON = 1e-05
LOG2_E = 1.4426950408889634
MESH = pl.DeviceIdType.MESH
PLANE = 4
RING = 4
COLUMN = 4
SIDES = 2
HALVES = 2
PARTS = 4


def attention_kernel(
    q_ref, k_ref, v_ref, span_ref, lam_ref, gain_ref, w_ref, out_ref,
    q_all, k_all, v_all, v_turned, scores, sums, stats, pieces, landed, own_piece, turned_back, normed,
    w_all, a_out, a_in, b_out, b_in, a_mine, a2_out, a2_in, b2_out, b2_in, result,
    q1_send, q1_recv, k_send, k_recv, v_send, v_recv, q2_send, q2_recv,
    st_send, st_recv, o_send, o_recv, n_send, n_recv, local_sem,
    a_send, a_recv, b_send, b_recv, a2_send, a2_recv, b2_send, b2_recv,
):
    ctx = lax.axis_index("ctx")
    head = lax.axis_index("head")
    x = ctx // PLANE
    j = lax.rem(ctx, PLANE)
    y = head // SIDES
    side = lax.rem(head, SIDES)
    part_rows = q_all.shape[3]
    tile = PLANE * part_rows
    held = k_all.shape[1]
    tokens = PLANE * held
    near = tokens // HALVES
    value_width = v_all.shape[2]
    half = q_all.shape[4] // 2
    step = min(256, held)
    steps = near // step
    factor = (half ** -0.5) * LOG2_E
    half_tiles = PARTS * RING
    n_tiles = HALVES * half_tiles
    zp = j // 2
    core = lax.rem(j, 2)
    share = part_rows // (COLUMN * SIDES)
    columns = w_ref.shape[1]
    area = columns // 2
    fold = area // 2
    stripe = min(512, fold)
    wide = min(2048, area)

    def partner(k):
        return (2 * zp + 1 - core, 2 * (1 - zp) + core, PLANE - 1 - j)[k - 1]

    def plane_device(k):
        return (x * PLANE + partner(k), head)

    def ring_device(d):
        return (lax.rem(x + d, RING) * PLANE + j, head)

    def column_device(d):
        return (ctx, lax.rem(y + d, COLUMN) * SIDES + side)

    other_side = (ctx, y * SIDES + 1 - side)

    barrier = pltpu.get_barrier_semaphore()
    for d in range(1, PLANE):
        pl.semaphore_signal(barrier, inc=1, device_id=plane_device(d), device_id_type=MESH)
    for d in range(1, RING):
        pl.semaphore_signal(barrier, inc=1, device_id=ring_device(d), device_id_type=MESH)
    for d in range(1, COLUMN):
        pl.semaphore_signal(barrier, inc=1, device_id=column_device(d), device_id_type=MESH)
    pl.semaphore_signal(barrier, inc=1, device_id=other_side, device_id_type=MESH)
    pl.semaphore_wait(barrier, PLANE + RING + COLUMN - 2)

    def q1(d, dst):
        return pltpu.make_async_remote_copy(
            q_ref.at[partner(d)], q_all.at[:, x, dst], q1_send.at[d], q1_recv.at[d],
            device_id=plane_device(d), device_id_type=MESH)

    def k1(d, dst):
        return pltpu.make_async_remote_copy(
            k_ref.at[partner(d)], k_all.at[dst], k_send.at[d], k_recv.at[d],
            device_id=plane_device(d), device_id_type=MESH)

    def v1(d, dst):
        return pltpu.make_async_remote_copy(
            v_ref.at[partner(d)], v_all.at[dst], v_send.at[d], v_recv.at[d],
            device_id=plane_device(d), device_id_type=MESH)

    def q2(r, d, dst, far):
        pair = pl.ds(2 * (1 - zp if far else zp), 2)
        at = (r * RING + d) * 2 + far
        return pltpu.make_async_remote_copy(
            q_all.at[r, x, pair], q_all.at[r, dst, pair], q2_send.at[at], q2_recv.at[at],
            device_id=ring_device(RING - d), device_id_type=MESH)

    def st(r, d, dst):
        return pltpu.make_async_remote_copy(
            stats.at[r, x], stats.at[r, dst], st_send.at[r * RING + d], st_recv.at[r * RING + d],
            device_id=ring_device(RING - d), device_id_type=MESH)

    def o1(r, d, dst):
        return pltpu.make_async_remote_copy(
            pieces.at[r, d], landed.at[r, dst], o_send.at[r * RING + d], o_recv.at[r * RING + d],
            device_id=ring_device(RING - d), device_id_type=MESH)

    def n1(r, d, dst):
        return pltpu.make_async_remote_copy(
            turned_back.at[r, partner(d)], normed.at[dst, r], n_send.at[r * PLANE + d], n_recv.at[r * PLANE + d],
            device_id=plane_device(d), device_id_type=MESH)

    def a1(r, d):
        return pltpu.make_async_remote_copy(
            a_out.at[r, lax.rem(y + d, COLUMN)], a_in.at[r, d], a_send.at[r * COLUMN + d], a_recv.at[r * COLUMN + d],
            device_id=column_device(d), device_id_type=MESH)

    def a2(r):
        return pltpu.make_async_remote_copy(
            a2_out.at[r], a2_in.at[r], a2_send.at[r], a2_recv.at[r], device_id=other_side, device_id_type=MESH)

    def b1(r):
        return pltpu.make_async_remote_copy(
            b_out.at[r, 1 - side], b_in.at[r], b_send.at[r], b_recv.at[r], device_id=other_side, device_id_type=MESH)

    def b2(r, d):
        return pltpu.make_async_remote_copy(
            b2_out.at[r, lax.rem(y + d, COLUMN)], b2_in.at[r, d], b2_send.at[r * COLUMN + d], b2_recv.at[r * COLUMN + d],
            device_id=column_device(d), device_id_type=MESH)

    def ring_source(d):
        return lax.rem(x + d, RING)

    def pass_on(r, far):
        for d in (1, 3, 2):
            q2(r, d, x, far).start()

    own_copies = [
        pltpu.make_async_copy(q_ref.at[j], q_all.at[:, x, j], local_sem.at[0]),
        pltpu.make_async_copy(k_ref.at[j], k_all.at[j], local_sem.at[1]),
        pltpu.make_async_copy(v_ref.at[j], v_all.at[j], local_sem.at[2]),
    ]
    own_copies[0].start()
    for d in (1, 2, 3):
        q1(d, j).start()
    for d in (2, 3, 1):
        k1(d, j).start()
        v1(d, j).start()
    own_copies[1].start()
    own_copies[2].start()
    weights_copy = pltpu.make_async_copy(w_ref, w_all, local_sem.at[3])
    weights_copy.start()
    own_copies[0].wait()
    q1(1, partner(1)).wait_recv()
    pass_on(0, 0)
    pass_on(1, 0)

    def clear(i, carry):
        r, plane = i // RING, lax.rem(i, RING)
        sums[r, plane] = jnp.zeros(sums.shape[2:], jnp.float32)
        lanes = pl.ds(pl.multiple_of(plane * tile, tile), tile)
        for m in range(2):
            stats[r, x, 2 * m:2 * m + 1, lanes] = jnp.full((1, tile), TOP_START, jnp.float32)
            stats[r, x, 2 * m + 1:2 * m + 2, lanes] = jnp.zeros((1, tile), jnp.float32)
        return carry

    lax.fori_loop(0, half_tiles, clear, 0)
    for d in (2, 3):
        q1(d, partner(d)).wait_recv()
    pass_on(0, 1)
    pass_on(1, 1)
    for r in range(2, PARTS):
        pass_on(r, 0)
        pass_on(r, 1)
    own_copies[1].wait()
    own_copies[2].wait()
    k1(1, partner(1)).wait_recv()
    v1(1, partner(1)).wait_recv()
    for source in (j, partner(1)):
        v_turned[source] = v_all[source].T

    def place(n):
        late = n // half_tiles
        at = lax.rem(n, half_tiles)
        return 2 * (zp + late - 2 * zp * late), at // RING, lax.rem(x + lax.rem(at, RING), RING)

    def score_step(n, m, t, slot, top):
        source, r, plane = place(n)
        query = q_all[r, plane, :, :, m * half:(m + 1) * half].reshape(tile, half)
        lanes = pl.ds(pl.multiple_of((r * RING + plane) * tile, tile), tile)
        base = x * tokens + source * held
        low = span_ref[0:1, lanes] - base
        high = span_ref[1:2, lanes] - base
        first = t * step
        key = k_all[source + first // held, first % held:first % held + step, m * half:(m + 1) * half]
        s = lax.dot_general(key, query, (((1,), (1,)), ((), ())), preferred_element_type=jnp.float32)
        at = lax.broadcasted_iota(jnp.int32, (step, tile), 0) + first
        s = jnp.where((at >= low) & (at < high), s, NEG_BIG)
        scores[slot, first:first + step, :] = s
        return jnp.maximum(top, jnp.max(s, axis=0, keepdims=True))

    def weight_step(n, t, slot, shift, total, summed):
        source, _, _ = place(n)
        first = t * step
        w = jnp.exp2(scores[slot, first:first + step, :] * factor - shift)
        total = total + jnp.sum(w, axis=0, keepdims=True)
        part = jnp.dot(
            v_turned[source + first // held, :, first % held:first % held + step], w.astype(jnp.bfloat16),
            preferred_element_type=jnp.float32)
        return total, (part if summed is None else summed + part)

    def send_stats(r):
        for d in range(1, RING):
            st(r, d, x).start()

    def combine(r):
        for d in range(1, RING):
            st(r, d, ring_source(d)).wait_recv()
        lam = lam_ref[j]
        for d in (1, 3, 2, 0):
            plane = lax.rem(x + RING - d, RING)
            lanes = pl.ds(pl.multiple_of(plane * tile, tile), tile)
            shares = []
            for m in range(2):
                tops = [stats[r, s, 2 * m:2 * m + 1, lanes] for s in range(RING)]
                totals = [stats[r, s, 2 * m + 1:2 * m + 2, lanes] for s in range(RING)]
                top = functools.reduce(jnp.maximum, tops)
                total = sum(a * jnp.exp2((b - top) * factor) for a, b in zip(totals, tops))
                own_top = stats[r, x, 2 * m:2 * m + 1, lanes]
                shares.append(jnp.exp2((own_top - top) * factor) / total)
            piece = sums[r, plane, 0] * shares[0] - sums[r, plane, 1] * (shares[1] * lam)
            if d == 0:
                own_piece[r] = piece
            else:
                pieces[r, d] = piece.astype(jnp.bfloat16)
                o1(r, d, d).start()

    def finish(r):
        for d in range(1, RING):
            o1(r, d, d).wait_recv()
        attended = own_piece[r]
        for d in range(1, RING):
            attended = attended + landed[r, d].astype(jnp.float32)
        mean_sq = jnp.mean(attended * attended, axis=0, keepdims=True)
        turned = (attended * lax.rsqrt(mean_sq + EPSILON)).T
        turned = turned * gain_ref[pl.ds(j, 1), :] * (1.0 - LAMBDA_INIT)
        turned_back[r] = turned.astype(jnp.bfloat16).reshape(PLANE, part_rows, value_width)
        for d in range(1, PLANE):
            n1(r, d, j).start()
        normed[j, r] = turned_back[r, j]

    def project(r):
        for d in range(1, PLANE):
            n1(r, d, partner(d)).wait_recv()
        rows = jnp.concatenate([normed[h, r] for h in range(PLANE)], axis=1)

        def product(first):
            return jnp.dot(rows, w_all[:, pl.ds(pl.multiple_of(first, wide), wide)], preferred_element_type=jnp.float32)

        def b_wide(i, carry):
            at = pl.ds(pl.multiple_of(i * wide, wide), wide)
            got = product(area + i * wide).astype(jnp.bfloat16)
            for side_to in range(SIDES):
                b_out[r, side_to, :, at] = got[side_to * COLUMN * share:(side_to + 1) * COLUMN * share]
            return carry

        def a_wide(i, carry):
            at = pl.ds(pl.multiple_of(i * wide, wide), wide)
            got = product(i * wide)
            for y_to in range(COLUMN):
                a_out[r, y_to, :, at] = jnp.concatenate(
                    [got[(s * COLUMN + y_to) * share:(s * COLUMN + y_to + 1) * share] for s in range(SIDES)], axis=0
                ).astype(jnp.bfloat16)
            return carry

        lax.fori_loop(0, area // wide, b_wide, 0)
        b1(r).start()
        lax.fori_loop(0, area // wide, a_wide, 0)
        for d in (1, 3, 2):
            a1(r, d).start()

    def add_first(r):
        b1(r).wait_recv()

        def b_stripe(i, carry):
            halves = []
            for k in range(2):
                at = pl.ds(pl.multiple_of(k * fold + i * stripe, stripe), stripe)
                halves.append(b_out[r, side, :, at].astype(jnp.float32) + b_in[r, :, at].astype(jnp.float32))
            at = pl.ds(pl.multiple_of(i * stripe, stripe), stripe)
            for y_to in range(COLUMN):
                b2_out[r, y_to, :, at] = jnp.concatenate(
                    [got[y_to * share:(y_to + 1) * share] for got in halves], axis=0).astype(jnp.bfloat16)
            return carry

        lax.fori_loop(0, fold // stripe, b_stripe, 0)
        for d in (1, 3, 2):
            b2(r, d).start()
        for d in range(1, COLUMN):
            a1(r, d).wait_recv()

        def a_stripe(i, carry):
            others = []
            for k in range(2):
                at = pl.ds(pl.multiple_of(k * fold + i * stripe, stripe), stripe)
                got = a_out[r, y, :, at].astype(jnp.float32)
                for d in range(1, COLUMN):
                    got = got + a_in[r, d, :, at].astype(jnp.float32)
                a_mine[r, :, at] = jnp.where(side == 0, got[:share], got[share:])
                others.append(jnp.where(side == 0, got[share:], got[:share]))
            at = pl.ds(pl.multiple_of(i * stripe, stripe), stripe)
            a2_out[r, :, at] = jnp.concatenate(others, axis=0).astype(jnp.bfloat16)
            return carry

        lax.fori_loop(0, fold // stripe, a_stripe, 0)
        a2(r).start()

    def add_last(r):
        for d in range(1, COLUMN):
            b2(r, d).wait_recv()
        a2(r).wait_recv()

        def last_stripe(i, carry):
            at = pl.ds(pl.multiple_of(i * stripe, stripe), stripe)
            a_got = a2_in[r, :, at].astype(jnp.float32)
            b_got = b2_out[r, y, :, at].astype(jnp.float32)
            for d in range(1, COLUMN):
                b_got = b_got + b2_in[r, d, :, at].astype(jnp.float32)
            for k in range(2):
                rows = slice(k * share, (k + 1) * share)
                here = pl.ds(pl.multiple_of(k * fold + i * stripe, stripe), stripe)
                result[r, :, here] = a_mine[r, :, here] + a_got[rows]
                there = pl.ds(pl.multiple_of(area + k * fold + i * stripe, stripe), stripe)
                result[r, :, there] = b_got[rows]
            return carry

        lax.fori_loop(0, fold // stripe, last_stripe, 0)

    stages = ((send_stats, 19), (combine, 24), (finish, 32), (project, 36), (add_first, 39), (add_last, 45))

    def run_stages(n):
        for stage, lag in reversed(stages):
            @pl.when((n >= lag) & (n < lag + PARTS * RING) & (lax.rem(n + 16 * RING - lag, RING) == 0))
            def _():
                stage((n - lag) // RING)

    def start_top(n, m):
        _, r, plane = place(n)
        return stats[r, x, 2 * m:2 * m + 1, pl.ds(pl.multiple_of(plane * tile, tile), tile)]

    top = start_top(0, 0)
    for t in range(steps):
        top = score_step(0, 0, t, 0, top)

    def body(n, top):
        _, r, plane = place(n)
        later = jnp.minimum(n + 1, n_tiles - 1)
        later_d = lax.rem(later, RING)

        @pl.when((n + 1 < half_tiles) & (later_d > 0))
        def _():
            for far in range(2):
                q2(later // RING, later_d, ring_source(later_d), far).wait_recv()

        @pl.when(n + 1 == half_tiles)
        def _():
            for d in (2, 3):
                k1(d, partner(d)).wait_recv()
                v1(d, partner(d)).wait_recv()
                v_turned[partner(d)] = v_all[partner(d)].T
            weights_copy.wait()

        lanes = pl.ds(pl.multiple_of(plane * tile, tile), tile)
        for m in range(2):
            following = n if m == 0 else later
            next_top = start_top(following, 1 - m)
            total = jnp.zeros((1, tile), jnp.float32)
            summed = None
            shift = top * factor
            for t in range(steps):
                next_top = score_step(following, 1 - m, t, 1 - m, next_top)
                total, summed = weight_step(n, t, m, shift, total, summed)
            kept = jnp.exp2((stats[r, x, 2 * m:2 * m + 1, lanes] - top) * factor)
            sums[r, plane, m] = sums[r, plane, m] * kept + summed
            stats[r, x, 2 * m:2 * m + 1, lanes] = top
            stats[r, x, 2 * m + 1:2 * m + 2, lanes] = stats[r, x, 2 * m + 1:2 * m + 2, lanes] * kept + total
            top = next_top

        run_stages(n)
        return top

    lax.fori_loop(0, n_tiles, body, top)

    def tail(n, carry):
        run_stages(n)
        return carry

    lax.fori_loop(n_tiles, stages[-1][1] + PARTS * RING, tail, 0)

    def last_waits(r, carry):
        for d in range(1, PLANE):
            n1(r, d, j).wait_send()
        for d in range(1, RING):
            q2(r, d, x, 0).wait_send()
            q2(r, d, x, 1).wait_send()
            st(r, d, x).wait_send()
            o1(r, d, d).wait_send()
        for d in range(1, COLUMN):
            a1(r, d).wait_send()
            b2(r, d).wait_send()
        a2(r).wait_send()
        b1(r).wait_send()
        return carry

    lax.fori_loop(0, PARTS, last_waits, 0)
    for d in range(1, PLANE):
        q1(d, j).wait_send()
        k1(d, j).wait_send()
        v1(d, j).wait_send()
    for i in range(columns // stripe):
        at = slice(i * stripe, (i + 1) * stripe)
        out_ref[:, at] = jnp.concatenate([result[r, :, at] for r in range(PARTS)], axis=0).astype(jnp.bfloat16)


def layer(queries, keys, values, spans, lambdas, gain, weights):
    heads, parts, part_rows, width = queries.shape
    held, value_width = values.shape[1:]
    tile = PLANE * part_rows
    tokens = PLANE * held
    vmem = pl.BlockSpec(memory_space=pltpu.VMEM)
    hbm = pl.BlockSpec(memory_space=pl.ANY)
    bf16, f32 = jnp.bfloat16, jnp.float32
    share = part_rows // (COLUMN * SIDES)
    columns = weights.shape[1]
    area = columns // 2
    dma = pltpu.SemaphoreType.DMA
    return pl.pallas_call(
        attention_kernel,
        out_shape=jax.ShapeDtypeStruct((parts * share, columns), bf16),
        in_specs=[hbm, hbm, hbm, vmem, pl.BlockSpec(memory_space=pltpu.SMEM), vmem, hbm],
        out_specs=vmem,
        scratch_shapes=[
            pltpu.VMEM((PARTS, RING, PLANE, part_rows, width), bf16),
            pltpu.VMEM((PLANE, held, width), bf16),
            pltpu.VMEM((PLANE, held, value_width), bf16),
            pltpu.VMEM((PLANE, value_width, held), bf16),
            pltpu.VMEM((2, tokens // HALVES, tile), f32),
            pltpu.VMEM((PARTS, RING, 2, value_width, tile), f32),
            pltpu.VMEM((PARTS, RING, 8, RING * tile), f32),
            pltpu.VMEM((PARTS, RING, value_width, tile), bf16),
            pltpu.VMEM((PARTS, RING, value_width, tile), bf16),
            pltpu.VMEM((PARTS, value_width, tile), f32),
            pltpu.VMEM((PARTS, PLANE, part_rows, value_width), bf16),
            pltpu.VMEM((PLANE, PARTS, part_rows, value_width), bf16),
            pltpu.VMEM(weights.shape, bf16),
            pltpu.VMEM((PARTS, COLUMN, SIDES * share, area), bf16),
            pltpu.VMEM((PARTS, COLUMN, SIDES * share, area), bf16),
            pltpu.VMEM((PARTS, SIDES, COLUMN * share, area), bf16),
            pltpu.VMEM((PARTS, COLUMN * share, area), bf16),
            pltpu.VMEM((PARTS, share, area), f32),
            pltpu.VMEM((PARTS, 2 * share, area // 2), bf16),
            pltpu.VMEM((PARTS, 2 * share, area // 2), bf16),
            pltpu.VMEM((PARTS, COLUMN, 2 * share, area // 2), bf16),
            pltpu.VMEM((PARTS, COLUMN, 2 * share, area // 2), bf16),
            pltpu.VMEM((PARTS, share, columns), f32),
            dma((PLANE,)), dma((PLANE,)), dma((PLANE,)), dma((PLANE,)), dma((PLANE,)), dma((PLANE,)),
            dma((2 * PARTS * RING,)), dma((2 * PARTS * RING,)), dma((PARTS * RING,)), dma((PARTS * RING,)),
            dma((PARTS * RING,)), dma((PARTS * RING,)), dma((PARTS * PLANE,)), dma((PARTS * PLANE,)),
            dma((4,)),
            dma((PARTS * COLUMN,)), dma((PARTS * COLUMN,)), dma((PARTS,)), dma((PARTS,)),
            dma((PARTS,)), dma((PARTS,)), dma((PARTS * COLUMN,)), dma((PARTS * COLUMN,)),
        ],
        compiler_params=pltpu.CompilerParams(
            collective_id=0, has_side_effects=True, vmem_limit_bytes=60 * 1024 * 1024),
    )(queries, keys, values, spans, lambdas, gain, weights)


def per_device(
    queries, cache_keys, cache_values, positions, doc_spans, lambdas, norm_gain, out_weight
):
    q_rows, heads_here, both_width = queries.shape
    part_rows = q_rows // PARTS
    share = part_rows // (COLUMN * SIDES)
    by_head = lambda a: jnp.transpose(a, (1, 0, 2))
    asked = queries.reshape(COLUMN, SIDES, PARTS, share, heads_here, both_width).transpose(4, 2, 1, 0, 3, 5)
    asked = asked.reshape(heads_here, PARTS, part_rows, both_width)
    spans = jnp.stack([doc_spans[:, 0] * BLK, jnp.minimum(positions + 1, doc_spans[:, 1] * BLK)])
    spans = spans.reshape(2, RING, PLANE, COLUMN, SIDES, PARTS, share).transpose(0, 5, 1, 2, 4, 3, 6).reshape(2, -1)
    return layer(
        asked, by_head(cache_keys), by_head(cache_values), spans, lambdas, norm_gain, out_weight)


def solution(mesh):
    placed = (
        P("ctx", "head", None),
        P("ctx", "head", None),
        P("ctx", "head", None),
        P(),
        P(),
        P("head"),
        P("head", None),
        P("head", None),
    )
    return jax.shard_map(
        per_device, mesh=mesh, in_specs=placed, out_specs=P(("ctx", "head"), None), check_vma=False
    )
```

```python
import functools

import jax
import jax.numpy as jnp
from jax import lax
from jax.experimental import pallas as pl
from jax.experimental.pallas import tpu as pltpu
from jax.sharding import PartitionSpec as P

BLK = 128
NEG_BIG = -1e30
TOP_START = -1e29
LAMBDA_INIT = 0.8
EPSILON = 1e-05
LOG2_E = 1.4426950408889634
MESH = pl.DeviceIdType.MESH
PLANE = 4
RING = 4
COLUMN = 4
SIDES = 2
HALVES = 2
PARTS = 4


def attention_kernel(
    q_ref, k_ref, v_ref, span_ref, lam_ref, gain_ref, w_ref, out_ref,
    q_all, k_all, v_all, v_turned, scores, sums, stats, pieces, landed, own_piece, turned_back, normed,
    w_all, a_out, a_in, b_out, b_in, a_mine, a2_out, a2_in, b2_out, b2_in, result,
    q1_send, q1_recv, k_send, k_recv, v_send, v_recv, q2_send, q2_recv,
    st_send, st_recv, o_send, o_recv, n_send, n_recv, local_sem,
    a_send, a_recv, b_send, b_recv, a2_send, a2_recv, b2_send, b2_recv,
):
    ctx = lax.axis_index("ctx")
    head = lax.axis_index("head")
    x = ctx // PLANE
    j = lax.rem(ctx, PLANE)
    y = head // SIDES
    side = lax.rem(head, SIDES)
    part_rows = q_all.shape[3]
    tile = PLANE * part_rows
    held = k_all.shape[1]
    tokens = PLANE * held
    near = tokens // HALVES
    value_width = v_all.shape[2]
    half = q_all.shape[4] // 2
    step = min(256, held)
    steps = near // step
    factor = (half ** -0.5) * LOG2_E
    half_tiles = PARTS * RING
    n_tiles = HALVES * half_tiles
    zp = j // 2
    core = lax.rem(j, 2)
    share = part_rows // (COLUMN * SIDES)
    columns = w_ref.shape[1]
    area = columns // 2
    fold = area // 2
    stripe = min(512, fold)
    wide = min(2048, area)

    def partner(k):
        return (2 * zp + 1 - core, 2 * (1 - zp) + core, PLANE - 1 - j)[k - 1]

    def plane_device(k):
        return (x * PLANE + partner(k), head)

    def ring_device(d):
        return (lax.rem(x + d, RING) * PLANE + j, head)

    def column_device(d):
        return (ctx, lax.rem(y + d, COLUMN) * SIDES + side)

    other_side = (ctx, y * SIDES + 1 - side)

    barrier = pltpu.get_barrier_semaphore()
    for d in range(1, PLANE):
        pl.semaphore_signal(barrier, inc=1, device_id=plane_device(d), device_id_type=MESH)
    for d in range(1, RING):
        pl.semaphore_signal(barrier, inc=1, device_id=ring_device(d), device_id_type=MESH)
    for d in range(1, COLUMN):
        pl.semaphore_signal(barrier, inc=1, device_id=column_device(d), device_id_type=MESH)
    pl.semaphore_signal(barrier, inc=1, device_id=other_side, device_id_type=MESH)
    pl.semaphore_wait(barrier, PLANE + RING + COLUMN - 2)

    def q1(d, dst):
        return pltpu.make_async_remote_copy(
            q_ref.at[partner(d)], q_all.at[:, x, dst], q1_send.at[d], q1_recv.at[d],
            device_id=plane_device(d), device_id_type=MESH)

    def k1(d, dst):
        return pltpu.make_async_remote_copy(
            k_ref.at[partner(d)], k_all.at[dst], k_send.at[d], k_recv.at[d],
            device_id=plane_device(d), device_id_type=MESH)

    def v1(d, dst):
        return pltpu.make_async_remote_copy(
            v_ref.at[partner(d)], v_all.at[dst], v_send.at[d], v_recv.at[d],
            device_id=plane_device(d), device_id_type=MESH)

    def q2(r, d, dst, far):
        pair = pl.ds(2 * (1 - zp if far else zp), 2)
        at = (r * RING + d) * 2 + far
        return pltpu.make_async_remote_copy(
            q_all.at[r, x, pair], q_all.at[r, dst, pair], q2_send.at[at], q2_recv.at[at],
            device_id=ring_device(RING - d), device_id_type=MESH)

    def st(r, d, dst):
        return pltpu.make_async_remote_copy(
            stats.at[r, x], stats.at[r, dst], st_send.at[r * RING + d], st_recv.at[r * RING + d],
            device_id=ring_device(RING - d), device_id_type=MESH)

    def o1(r, d, dst):
        return pltpu.make_async_remote_copy(
            pieces.at[r, d], landed.at[r, dst], o_send.at[r * RING + d], o_recv.at[r * RING + d],
            device_id=ring_device(RING - d), device_id_type=MESH)

    def n1(r, d, dst):
        return pltpu.make_async_remote_copy(
            turned_back.at[r, partner(d)], normed.at[dst, r], n_send.at[r * PLANE + d], n_recv.at[r * PLANE + d],
            device_id=plane_device(d), device_id_type=MESH)

    def a1(r, d):
        return pltpu.make_async_remote_copy(
            a_out.at[r, lax.rem(y + d, COLUMN)], a_in.at[r, d], a_send.at[r * COLUMN + d], a_recv.at[r * COLUMN + d],
            device_id=column_device(d), device_id_type=MESH)

    def a2(r):
        return pltpu.make_async_remote_copy(
            a2_out.at[r], a2_in.at[r], a2_send.at[r], a2_recv.at[r], device_id=other_side, device_id_type=MESH)

    def b1(r):
        return pltpu.make_async_remote_copy(
            b_out.at[r, 1 - side], b_in.at[r], b_send.at[r], b_recv.at[r], device_id=other_side, device_id_type=MESH)

    def b2(r, d):
        return pltpu.make_async_remote_copy(
            b2_out.at[r, lax.rem(y + d, COLUMN)], b2_in.at[r, d], b2_send.at[r * COLUMN + d], b2_recv.at[r * COLUMN + d],
            device_id=column_device(d), device_id_type=MESH)

    def ring_source(d):
        return lax.rem(x + d, RING)

    def pass_on(r, far):
        for d in (1, 3, 2):
            q2(r, d, x, far).start()

    own_copies = [
        pltpu.make_async_copy(q_ref.at[j], q_all.at[:, x, j], local_sem.at[0]),
        pltpu.make_async_copy(k_ref.at[j], k_all.at[j], local_sem.at[1]),
        pltpu.make_async_copy(v_ref.at[j], v_all.at[j], local_sem.at[2]),
    ]
    own_copies[0].start()
    for d in (1, 2, 3):
        q1(d, j).start()
    for d in (1, 2, 3):
        k1(d, j).start()
        v1(d, j).start()
    own_copies[1].start()
    own_copies[2].start()
    weights_copy = pltpu.make_async_copy(w_ref, w_all, local_sem.at[3])
    weights_copy.start()
    own_copies[0].wait()
    q1(1, partner(1)).wait_recv()
    pass_on(0, 0)
    pass_on(1, 0)

    def clear(i, carry):
        r, plane = i // RING, lax.rem(i, RING)
        sums[r, plane] = jnp.zeros(sums.shape[2:], jnp.float32)
        lanes = pl.ds(pl.multiple_of(plane * tile, tile), tile)
        for m in range(2):
            stats[r, x, 2 * m:2 * m + 1, lanes] = jnp.full((1, tile), TOP_START, jnp.float32)
            stats[r, x, 2 * m + 1:2 * m + 2, lanes] = jnp.zeros((1, tile), jnp.float32)
        return carry

    lax.fori_loop(0, half_tiles, clear, 0)
    for d in (2, 3):
        q1(d, partner(d)).wait_recv()
    pass_on(0, 1)
    pass_on(1, 1)
    for r in range(2, PARTS):
        pass_on(r, 0)
        pass_on(r, 1)
    own_copies[1].wait()
    own_copies[2].wait()
    k1(1, partner(1)).wait_recv()
    v1(1, partner(1)).wait_recv()
    for source in (j, partner(1)):
        v_turned[source] = v_all[source].T

    def place(n):
        late = n // half_tiles
        at = lax.rem(n, half_tiles)
        return 2 * (zp + late - 2 * zp * late), at // RING, lax.rem(x + lax.rem(at, RING), RING)

    def score_step(n, m, t, slot, top):
        source, r, plane = place(n)
        query = q_all[r, plane, :, :, m * half:(m + 1) * half].reshape(tile, half)
        lanes = pl.ds(pl.multiple_of((r * RING + plane) * tile, tile), tile)
        base = x * tokens + source * held
        low = span_ref[0:1, lanes] - base
        high = span_ref[1:2, lanes] - base
        first = t * step
        key = k_all[source + first // held, first % held:first % held + step, m * half:(m + 1) * half]
        s = lax.dot_general(key, query, (((1,), (1,)), ((), ())), preferred_element_type=jnp.float32)
        at = lax.broadcasted_iota(jnp.int32, (step, tile), 0) + first
        s = jnp.where((at >= low) & (at < high), s, NEG_BIG)
        scores[slot, first:first + step, :] = s
        return jnp.maximum(top, jnp.max(s, axis=0, keepdims=True))

    def weight_step(n, t, slot, shift, total, summed):
        source, _, _ = place(n)
        first = t * step
        w = jnp.exp2(scores[slot, first:first + step, :] * factor - shift)
        total = total + jnp.sum(w, axis=0, keepdims=True)
        part = jnp.dot(
            v_turned[source + first // held, :, first % held:first % held + step], w.astype(jnp.bfloat16),
            preferred_element_type=jnp.float32)
        return total, (part if summed is None else summed + part)

    def send_stats(r):
        for d in range(1, RING):
            st(r, d, x).start()

    def combine(r):
        for d in range(1, RING):
            st(r, d, ring_source(d)).wait_recv()
        lam = lam_ref[j]
        for d in (1, 3, 2, 0):
            plane = lax.rem(x + RING - d, RING)
            lanes = pl.ds(pl.multiple_of(plane * tile, tile), tile)
            shares = []
            for m in range(2):
                tops = [stats[r, s, 2 * m:2 * m + 1, lanes] for s in range(RING)]
                totals = [stats[r, s, 2 * m + 1:2 * m + 2, lanes] for s in range(RING)]
                top = functools.reduce(jnp.maximum, tops)
                total = sum(a * jnp.exp2((b - top) * factor) for a, b in zip(totals, tops))
                own_top = stats[r, x, 2 * m:2 * m + 1, lanes]
                shares.append(jnp.exp2((own_top - top) * factor) / total)
            piece = sums[r, plane, 0] * shares[0] - sums[r, plane, 1] * (shares[1] * lam)
            if d == 0:
                own_piece[r] = piece
            else:
                pieces[r, d] = piece.astype(jnp.bfloat16)
                o1(r, d, d).start()

    def finish(r):
        for d in range(1, RING):
            o1(r, d, d).wait_recv()
        attended = own_piece[r]
        for d in range(1, RING):
            attended = attended + landed[r, d].astype(jnp.float32)
        mean_sq = jnp.mean(attended * attended, axis=0, keepdims=True)
        turned = (attended * lax.rsqrt(mean_sq + EPSILON)).T
        turned = turned * gain_ref[pl.ds(j, 1), :] * (1.0 - LAMBDA_INIT)
        turned_back[r] = turned.astype(jnp.bfloat16).reshape(PLANE, part_rows, value_width)
        for d in range(1, PLANE):
            n1(r, d, j).start()
        normed[j, r] = turned_back[r, j]

    def project(r):
        for d in range(1, PLANE):
            n1(r, d, partner(d)).wait_recv()
        rows = jnp.concatenate([normed[h, r] for h in range(PLANE)], axis=1)

        def product(first):
            return jnp.dot(rows, w_all[:, pl.ds(pl.multiple_of(first, wide), wide)], preferred_element_type=jnp.float32)

        def b_wide(i, carry):
            at = pl.ds(pl.multiple_of(i * wide, wide), wide)
            got = product(area + i * wide).astype(jnp.bfloat16)
            for side_to in range(SIDES):
                b_out[r, side_to, :, at] = got[side_to * COLUMN * share:(side_to + 1) * COLUMN * share]
            return carry

        def a_wide(i, carry):
            at = pl.ds(pl.multiple_of(i * wide, wide), wide)
            got = product(i * wide)
            for y_to in range(COLUMN):
                a_out[r, y_to, :, at] = jnp.concatenate(
                    [got[(s * COLUMN + y_to) * share:(s * COLUMN + y_to + 1) * share] for s in range(SIDES)], axis=0
                ).astype(jnp.bfloat16)
            return carry

        lax.fori_loop(0, area // wide, b_wide, 0)
        b1(r).start()
        lax.fori_loop(0, area // wide, a_wide, 0)
        for d in (1, 3, 2):
            a1(r, d).start()

    def add_first(r):
        b1(r).wait_recv()

        def b_stripe(i, carry):
            halves = []
            for k in range(2):
                at = pl.ds(pl.multiple_of(k * fold + i * stripe, stripe), stripe)
                halves.append(b_out[r, side, :, at].astype(jnp.float32) + b_in[r, :, at].astype(jnp.float32))
            at = pl.ds(pl.multiple_of(i * stripe, stripe), stripe)
            for y_to in range(COLUMN):
                b2_out[r, y_to, :, at] = jnp.concatenate(
                    [got[y_to * share:(y_to + 1) * share] for got in halves], axis=0).astype(jnp.bfloat16)
            return carry

        lax.fori_loop(0, fold // stripe, b_stripe, 0)
        for d in (1, 3, 2):
            b2(r, d).start()
        for d in range(1, COLUMN):
            a1(r, d).wait_recv()

        def a_stripe(i, carry):
            others = []
            for k in range(2):
                at = pl.ds(pl.multiple_of(k * fold + i * stripe, stripe), stripe)
                got = a_out[r, y, :, at].astype(jnp.float32)
                for d in range(1, COLUMN):
                    got = got + a_in[r, d, :, at].astype(jnp.float32)
                a_mine[r, :, at] = jnp.where(side == 0, got[:share], got[share:])
                others.append(jnp.where(side == 0, got[share:], got[:share]))
            at = pl.ds(pl.multiple_of(i * stripe, stripe), stripe)
            a2_out[r, :, at] = jnp.concatenate(others, axis=0).astype(jnp.bfloat16)
            return carry

        lax.fori_loop(0, fold // stripe, a_stripe, 0)
        a2(r).start()

    def add_last(r):
        for d in range(1, COLUMN):
            b2(r, d).wait_recv()
        a2(r).wait_recv()

        def last_stripe(i, carry):
            at = pl.ds(pl.multiple_of(i * stripe, stripe), stripe)
            a_got = a2_in[r, :, at].astype(jnp.float32)
            b_got = b2_out[r, y, :, at].astype(jnp.float32)
            for d in range(1, COLUMN):
                b_got = b_got + b2_in[r, d, :, at].astype(jnp.float32)
            for k in range(2):
                rows = slice(k * share, (k + 1) * share)
                here = pl.ds(pl.multiple_of(k * fold + i * stripe, stripe), stripe)
                result[r, :, here] = a_mine[r, :, here] + a_got[rows]
                there = pl.ds(pl.multiple_of(area + k * fold + i * stripe, stripe), stripe)
                result[r, :, there] = b_got[rows]
            return carry

        lax.fori_loop(0, fold // stripe, last_stripe, 0)

    stages = ((send_stats, 19), (combine, 24), (finish, 32), (project, 36), (add_first, 39), (add_last, 45))

    def run_stages(n):
        for stage, lag in reversed(stages):
            @pl.when((n >= lag) & (n < lag + PARTS * RING) & (lax.rem(n + 16 * RING - lag, RING) == 0))
            def _():
                stage((n - lag) // RING)

    def start_top(n, m):
        _, r, plane = place(n)
        return stats[r, x, 2 * m:2 * m + 1, pl.ds(pl.multiple_of(plane * tile, tile), tile)]

    top = start_top(0, 0)
    for t in range(steps):
        top = score_step(0, 0, t, 0, top)

    def body(n, top):
        _, r, plane = place(n)
        later = jnp.minimum(n + 1, n_tiles - 1)
        later_d = lax.rem(later, RING)

        @pl.when((n + 1 < half_tiles) & (later_d > 0))
        def _():
            for far in range(2):
                q2(later // RING, later_d, ring_source(later_d), far).wait_recv()

        @pl.when(n + 1 == half_tiles)
        def _():
            for d in (2, 3):
                k1(d, partner(d)).wait_recv()
                v1(d, partner(d)).wait_recv()
                v_turned[partner(d)] = v_all[partner(d)].T
            weights_copy.wait()

        lanes = pl.ds(pl.multiple_of(plane * tile, tile), tile)
        for m in range(2):
            following = n if m == 0 else later
            next_top = start_top(following, 1 - m)
            total = jnp.zeros((1, tile), jnp.float32)
            summed = None
            shift = top * factor
            for t in range(steps):
                next_top = score_step(following, 1 - m, t, 1 - m, next_top)
                total, summed = weight_step(n, t, m, shift, total, summed)
            kept = jnp.exp2((stats[r, x, 2 * m:2 * m + 1, lanes] - top) * factor)
            sums[r, plane, m] = sums[r, plane, m] * kept + summed
            stats[r, x, 2 * m:2 * m + 1, lanes] = top
            stats[r, x, 2 * m + 1:2 * m + 2, lanes] = stats[r, x, 2 * m + 1:2 * m + 2, lanes] * kept + total
            top = next_top

        run_stages(n)
        return top

    lax.fori_loop(0, n_tiles, body, top)

    def tail(n, carry):
        run_stages(n)
        return carry

    lax.fori_loop(n_tiles, stages[-1][1] + PARTS * RING, tail, 0)

    def last_waits(r, carry):
        for d in range(1, PLANE):
            n1(r, d, j).wait_send()
        for d in range(1, RING):
            q2(r, d, x, 0).wait_send()
            q2(r, d, x, 1).wait_send()
            st(r, d, x).wait_send()
            o1(r, d, d).wait_send()
        for d in range(1, COLUMN):
            a1(r, d).wait_send()
            b2(r, d).wait_send()
        a2(r).wait_send()
        b1(r).wait_send()
        return carry

    lax.fori_loop(0, PARTS, last_waits, 0)
    for d in range(1, PLANE):
        q1(d, j).wait_send()
        k1(d, j).wait_send()
        v1(d, j).wait_send()
    for i in range(columns // stripe):
        at = slice(i * stripe, (i + 1) * stripe)
        out_ref[:, at] = jnp.concatenate([result[r, :, at] for r in range(PARTS)], axis=0).astype(jnp.bfloat16)


def layer(queries, keys, values, spans, lambdas, gain, weights):
    heads, parts, part_rows, width = queries.shape
    held, value_width = values.shape[1:]
    tile = PLANE * part_rows
    tokens = PLANE * held
    vmem = pl.BlockSpec(memory_space=pltpu.VMEM)
    hbm = pl.BlockSpec(memory_space=pl.ANY)
    bf16, f32 = jnp.bfloat16, jnp.float32
    share = part_rows // (COLUMN * SIDES)
    columns = weights.shape[1]
    area = columns // 2
    dma = pltpu.SemaphoreType.DMA
    return pl.pallas_call(
        attention_kernel,
        out_shape=jax.ShapeDtypeStruct((parts * share, columns), bf16),
        in_specs=[hbm, hbm, hbm, vmem, pl.BlockSpec(memory_space=pltpu.SMEM), vmem, hbm],
        out_specs=vmem,
        scratch_shapes=[
            pltpu.VMEM((PARTS, RING, PLANE, part_rows, width), bf16),
            pltpu.VMEM((PLANE, held, width), bf16),
            pltpu.VMEM((PLANE, held, value_width), bf16),
            pltpu.VMEM((PLANE, value_width, held), bf16),
            pltpu.VMEM((2, tokens // HALVES, tile), f32),
            pltpu.VMEM((PARTS, RING, 2, value_width, tile), f32),
            pltpu.VMEM((PARTS, RING, 8, RING * tile), f32),
            pltpu.VMEM((PARTS, RING, value_width, tile), bf16),
            pltpu.VMEM((PARTS, RING, value_width, tile), bf16),
            pltpu.VMEM((PARTS, value_width, tile), f32),
            pltpu.VMEM((PARTS, PLANE, part_rows, value_width), bf16),
            pltpu.VMEM((PLANE, PARTS, part_rows, value_width), bf16),
            pltpu.VMEM(weights.shape, bf16),
            pltpu.VMEM((PARTS, COLUMN, SIDES * share, area), bf16),
            pltpu.VMEM((PARTS, COLUMN, SIDES * share, area), bf16),
            pltpu.VMEM((PARTS, SIDES, COLUMN * share, area), bf16),
            pltpu.VMEM((PARTS, COLUMN * share, area), bf16),
            pltpu.VMEM((PARTS, share, area), f32),
            pltpu.VMEM((PARTS, 2 * share, area // 2), bf16),
            pltpu.VMEM((PARTS, 2 * share, area // 2), bf16),
            pltpu.VMEM((PARTS, COLUMN, 2 * share, area // 2), bf16),
            pltpu.VMEM((PARTS, COLUMN, 2 * share, area // 2), bf16),
            pltpu.VMEM((PARTS, share, columns), f32),
            dma((PLANE,)), dma((PLANE,)), dma((PLANE,)), dma((PLANE,)), dma((PLANE,)), dma((PLANE,)),
            dma((2 * PARTS * RING,)), dma((2 * PARTS * RING,)), dma((PARTS * RING,)), dma((PARTS * RING,)),
            dma((PARTS * RING,)), dma((PARTS * RING,)), dma((PARTS * PLANE,)), dma((PARTS * PLANE,)),
            dma((4,)),
            dma((PARTS * COLUMN,)), dma((PARTS * COLUMN,)), dma((PARTS,)), dma((PARTS,)),
            dma((PARTS,)), dma((PARTS,)), dma((PARTS * COLUMN,)), dma((PARTS * COLUMN,)),
        ],
        compiler_params=pltpu.CompilerParams(
            collective_id=0, has_side_effects=True, vmem_limit_bytes=60 * 1024 * 1024),
    )(queries, keys, values, spans, lambdas, gain, weights)


def per_device(
    queries, cache_keys, cache_values, positions, doc_spans, lambdas, norm_gain, out_weight
):
    q_rows, heads_here, both_width = queries.shape
    part_rows = q_rows // PARTS
    share = part_rows // (COLUMN * SIDES)
    by_head = lambda a: jnp.transpose(a, (1, 0, 2))
    asked = queries.reshape(COLUMN, SIDES, PARTS, share, heads_here, both_width).transpose(4, 2, 1, 0, 3, 5)
    asked = asked.reshape(heads_here, PARTS, part_rows, both_width)
    spans = jnp.stack([doc_spans[:, 0] * BLK, jnp.minimum(positions + 1, doc_spans[:, 1] * BLK)])
    spans = spans.reshape(2, RING, PLANE, COLUMN, SIDES, PARTS, share).transpose(0, 5, 1, 2, 4, 3, 6).reshape(2, -1)
    return layer(
        asked, by_head(cache_keys), by_head(cache_values), spans, lambdas, norm_gain, out_weight)


def solution(mesh):
    placed = (
        P("ctx", "head", None),
        P("ctx", "head", None),
        P("ctx", "head", None),
        P(),
        P(),
        P("head"),
        P("head", None),
        P("head", None),
    )
    return jax.shard_map(
        per_device, mesh=mesh, in_specs=placed, out_specs=P(("ctx", "head"), None), check_vma=False
    )
```
